512 devices in a mesh: dx: 128 (over y, z_hi, x), dy: 4 (over z_lo, core).
Axes of the slice: x: 4, y: 8, z: 8 (z_hi: 4, z_lo: 2; z = z_hi * 2 + z_lo), core: 2. Of those that a mesh axis runs over, the one named last changes fastest.
Arguments:
- features: bfloat16 [65536, 128], P(('dx', 'dy')), may hold values from -6 to 6
- positions: float32 [3, 65536], P(None, ('dx', 'dy')), may hold values from 0 to 1, as said below
- neighbours: int32 [65536, 64], P(('dx', 'dy')), may hold values from 0 to 256, as said below
- distances: float32 [65536, 64], P(('dx', 'dy')), may hold values from 0.5 to 5
- ghost_rows: int32 [4, 16384], P(None, ('dx', 'dy')), may hold values from 0 to 127, as said below
- atom_counts: int32 [512], P(('dx', 'dy')), may hold values from 64 to 128, as said below
- wavevectors: float32 [3, 2048], replicated, may hold values from -40 to 40
- wave_weights: float32 [2048], replicated, may hold values from 0.05 to 1
- source_weight: bfloat16 [128, 128], replicated, may hold values from -0.5 to 0.5
- target_weight: bfloat16 [128, 128], replicated, may hold values from -0.5 to 0.5
- edge_weight: bfloat16 [128, 128], replicated, may hold values from -0.5 to 0.5
- mix_weight: bfloat16 [128, 128], replicated, may hold values from -0.0625 to 0.0625
- charge_weight: bfloat16 [128, 64], replicated, may hold values from -0.5 to 0.5
- field_weight: bfloat16 [64, 128], replicated, may hold values from -0.75 to 0.75
- cotangent: bfloat16 [65536, 128], P(('dx', 'dy')), may hold values from -6 to 6
Outputs:
- layer_output: bfloat16 [65536, 128], P(('dx', 'dy'))
- feature_grad: bfloat16 [65536, 128], P(('dx', 'dy'))
- source_grad: float32 [128, 128], replicated
- target_grad: float32 [128, 128], replicated
- edge_grad: float32 [128, 128], replicated
- mix_grad: float32 [128, 128], replicated
- charge_grad: float32 [128, 64], replicated
- field_grad: float32 [64, 128], replicated
The draws below stay inside these ranges and needn't reach their ends.
Inputs may be any that keep to these rules, and one draw needn't show every extreme that they name: `atom_counts`: each domain's count of live atoms; slots from that count on are padding. Some domain is full and some holds exactly half of 128. `neighbours`: an entry below 128 names a live atom of the row's own domain; 128 + f * 32 + g names ghost row g of block f of the domain's table; 256 marks an empty slot. `ghost_rows`: column block d of row f lists live atoms of domain d that it sends over face f (f = 0: to the domain after it along dx, 1: before it along dx, 2: after it along dy, 3: before it along dy, with wrap); rows may repeat. `positions`: each atom lies in its domain's part of the unit box: its first coordinate within [ix / 128, (ix + 1) / 128) and its second within [iy / 4, (iy + 1) / 4) for the domain's indices ix, iy.
All inputs are finite; a program needn't handle non-finite values.
Results may differ from the reference program's by a relative error of at most 0.011.
Values may be sent and summed in bfloat16 or wider, within the bound.
A program may use at most 64 MiB of HBM per device.

```python
import math
import jax
import jax.numpy as jnp
from jax import lax

C = 128
CL = 64
K = 2048
NB = 64
A_DEV = 128
GHOST = 32
ATOMS = 65536
N_DX = 128
N_DY = 4


def atom_counts_shared(key):
    key = jax.random.fold_in(key, 101)
    count_key, full_key, offset_key = jax.random.split(key, 3)
    domains = N_DX * N_DY
    counts = jax.random.randint(count_key, (domains,), A_DEV // 2, A_DEV + 1)
    fullest = jax.random.randint(full_key, (), 0, domains)
    offset = jax.random.randint(offset_key, (), 1, domains)
    emptiest = (fullest + offset) % domains
    domain_ids = jnp.arange(domains)
    counts = jnp.where(domain_ids == fullest, A_DEV, counts)
    return (jnp.where(domain_ids == emptiest, A_DEV // 2, counts).astype(jnp.int32), fullest)


def draw_atom_counts(key, part):
    counts, fullest = atom_counts_shared(key)
    return counts


def draw_neighbours(key, part):
    counts, fullest = atom_counts_shared(key)
    key = jax.random.fold_in(key, 2)
    kind_key, local_key, ghost_key = jax.random.split(key, 3)
    domain_of = jnp.arange(ATOMS) // A_DEV
    limit = counts[domain_of][:, None]
    kinds = jax.random.randint(kind_key, (ATOMS, NB), 0, 8)
    local_ids = jax.random.randint(local_key, (ATOMS, NB), 0, limit)
    ghost_ids = A_DEV + jax.random.randint(ghost_key, (ATOMS, NB), 0, 4 * GHOST)
    chosen = jnp.where(kinds < 5, local_ids, jnp.where(kinds < 7, ghost_ids, A_DEV + 4 * GHOST))
    return chosen.astype(jnp.int32)


def draw_ghost_rows(key, part):
    counts, fullest = atom_counts_shared(key)
    key = jax.random.fold_in(key, 3)
    columns = GHOST * N_DX * N_DY
    limit = counts[jnp.arange(columns) // GHOST][None, :]
    picked = jax.random.randint(key, (4, columns), 0, limit)
    first_column = fullest * GHOST
    picked = picked.at[0, first_column].set(A_DEV - 1)
    picked = picked.at[1, first_column].set(0)
    return picked.astype(jnp.int32)


def draw_positions(key, part):
    key = jax.random.fold_in(key, 4)
    domain_of = jnp.arange(ATOMS) // A_DEV
    first_index = (domain_of // N_DY).astype(jnp.float32)
    second_index = (domain_of % N_DY).astype(jnp.float32)
    uniform = jax.random.uniform(key, (3, ATOMS), jnp.float32)
    first_coord = (first_index + uniform[0]) / N_DX
    second_coord = (second_index + uniform[1]) / N_DY
    return jnp.stack([first_coord, second_coord, uniform[2]], axis=0).astype(jnp.float32)


def shard_levels(rng, dims, shards, low, largest):
    level = 1.0
    for position, parts in shards:
        heights = jax.random.uniform(jax.random.fold_in(jax.random.fold_in(rng, 6), position), (parts,), jnp.float32, low / len(shards), largest / len(shards))
        level = level * jnp.repeat(jnp.exp(heights), dims[position] // parts).reshape((-1,) + (1,) * (len(dims) - 1 - position))
    return level


def noise(key, shape, spread, most, shards=(), kind=jnp.bfloat16):
    loudness = shard_levels(key, shape, shards, -0.22, 0.18) if shards else 1.0
    drawn = jax.random.normal(key, shape, jnp.float32) * spread * loudness
    return jnp.minimum(jnp.maximum(drawn, -most), most).astype(kind)


def setup_inputs(seed: int = 0) -> dict:
    streams_of = jax.random.split(jax.random.key(seed), 16)
    features = noise(streams_of[0], (ATOMS, C), 1.0, 6.0, ((0, 512),))
    positions = draw_positions(jax.random.fold_in(streams_of[15], 71), 0)
    neighbours = draw_neighbours(jax.random.fold_in(streams_of[15], 71), 0)
    distances = jnp.clip(0.5 + 4.5 * jax.random.uniform(streams_of[3], (ATOMS, NB), jnp.float32) ** shard_levels(streams_of[3], (ATOMS, NB), ((0, 512),), -0.2, 0.2), 0.5, 5.0)
    ghost_rows = draw_ghost_rows(jax.random.fold_in(streams_of[15], 71), 0)
    atom_counts = draw_atom_counts(jax.random.fold_in(streams_of[15], 71), 0)
    wavevectors = jnp.clip(jax.random.uniform(streams_of[6], (3, K), jnp.float32, -40.0, 40.0), -40.0, 40.0)
    wave_weights = jnp.clip(jnp.exp(jax.random.uniform(streams_of[7], (K,), jnp.float32, math.log(0.05), math.log(1.0))), 0.05, 1.0)
    source_weight = noise(streams_of[8], (C, C), C ** -0.5, 0.5)
    target_weight = noise(streams_of[9], (C, C), C ** -0.5, 0.5)
    edge_weight = noise(streams_of[10], (C, C), C ** -0.5, 0.5)
    mix_weight = noise(streams_of[11], (C, C), (C * NB) ** -0.5, 0.0625)
    charge_weight = noise(streams_of[12], (C, CL), C ** -0.5, 0.5)
    field_weight = noise(streams_of[13], (CL, C), CL ** -0.5, 0.75)
    cotangent = noise(streams_of[14], (ATOMS, C), 1.0, 6.0, ((0, 512),))
    return dict(features=features, positions=positions, neighbours=neighbours, distances=distances, ghost_rows=ghost_rows, atom_counts=atom_counts, wavevectors=wavevectors, wave_weights=wave_weights, source_weight=source_weight, target_weight=target_weight, edge_weight=edge_weight, mix_weight=mix_weight, charge_weight=charge_weight, field_weight=field_weight, cotangent=cotangent)


cutoff_rate = math.pi / 5.0

def silu_slope(argument):
    logistic = jax.nn.sigmoid(argument)
    return logistic * (1.0 + argument * (1.0 - logistic))

def contract_rows(left_side, right_side):
    return lax.dot_general(left_side, right_side, (((0,), (0,)), ((), ())), preferred_element_type=jnp.float32)

def contract_cols(left_side, right_side):
    return lax.dot_general(left_side, right_side, (((1,), (1,)), ((), ())), preferred_element_type=jnp.float32)

def phases(coords, wave_table):
    phase_angle = coords[0][:, None] * wave_table[0][None, :] + coords[1][:, None] * wave_table[1][None, :] + coords[2][:, None] * wave_table[2][None, :]
    return (jnp.cos(phase_angle).astype(jnp.bfloat16), jnp.sin(phase_angle).astype(jnp.bfloat16))

def weigh_totals(totals, factor):
    return (totals * factor[:, None]).astype(jnp.bfloat16)

def edge_geometry(source, target_table, neighbour, distance):
    nearby = target_table[neighbour]
    summed = source[:, None, :].astype(jnp.float32) + nearby.astype(jnp.float32)
    validity = (neighbour < target_table.shape[0] - 1).astype(jnp.float32)
    edge_gate = validity * (0.5 + 0.5 * jnp.cos(distance * cutoff_rate))
    return (summed, edge_gate)

def edge_forward(source, target_table, neighbour, distance, edge_weight):
    summed, edge_gate = edge_geometry(source, target_table, neighbour, distance)
    hidden = jax.nn.silu(summed).astype(jnp.bfloat16)
    row_total = hidden.shape[0] * hidden.shape[1]
    mixed = jnp.dot(hidden.reshape(row_total, hidden.shape[2]), edge_weight, preferred_element_type=jnp.float32)
    message = jax.nn.silu(mixed).reshape(summed.shape)
    return lax.optimization_barrier(jnp.sum(edge_gate[:, :, None] * message, axis=1)).astype(jnp.bfloat16)

def edge_backward(source, target_table, neighbour, distance, edge_weight, upstream):
    summed, edge_gate = edge_geometry(source, target_table, neighbour, distance)
    hidden = jax.nn.silu(summed).astype(jnp.bfloat16)
    row_total = hidden.shape[0] * hidden.shape[1]
    hidden_flat = hidden.reshape(row_total, hidden.shape[2])
    mixed = jnp.dot(hidden_flat, edge_weight, preferred_element_type=jnp.float32)
    slopes = silu_slope(mixed).reshape(summed.shape)
    inner_grad = (edge_gate[:, :, None] * upstream[:, None, :].astype(jnp.float32) * slopes).astype(jnp.bfloat16)
    inner_flat = inner_grad.reshape(row_total, inner_grad.shape[2])
    edge_part = contract_rows(hidden_flat, inner_flat)
    outer_grad = contract_cols(inner_flat, edge_weight).reshape(summed.shape)
    pair_grad = (outer_grad * silu_slope(summed)).astype(jnp.bfloat16)
    source_part = lax.optimization_barrier(jnp.sum(pair_grad.astype(jnp.float32), axis=1))
    table_part = jnp.zeros((target_table.shape[0], pair_grad.shape[2]), jnp.float32).at[neighbour.reshape(-1)].add(pair_grad.reshape(row_total, pair_grad.shape[2]).astype(jnp.float32))
    return (edge_part, source_part, table_part)

def ewald(values, coords, wave_table, factor):

    def accumulate(running, block_items):
        cosine_rows, sine_rows = phases(block_items[1], wave_table)
        return ((running[0] + contract_rows(cosine_rows, block_items[0]), running[1] + contract_rows(sine_rows, block_items[0])), None)
    zero_sum = jnp.zeros((wave_table.shape[1], values.shape[2]), jnp.float32)
    totals, unused = lax.scan(accumulate, (zero_sum, zero_sum), (values, coords))
    weight_cos = weigh_totals(totals[0], factor)
    weight_sin = weigh_totals(totals[1], factor)

    def apply_field(coord_rows):
        cosine_rows, sine_rows = phases(coord_rows, wave_table)
        return (jnp.dot(cosine_rows, weight_cos, preferred_element_type=jnp.float32) + jnp.dot(sine_rows, weight_sin, preferred_element_type=jnp.float32)).astype(jnp.bfloat16)
    return lax.map(apply_field, coords)

def reference(features, positions, neighbours, distances, ghost_rows, atom_counts, wavevectors, wave_weights, source_weight, target_weight, edge_weight, mix_weight, charge_weight, field_weight, cotangent):
    domains = N_DX * N_DY
    slot_ids = jnp.arange(ATOMS, dtype=jnp.int32)
    alive_mask = (slot_ids % A_DEV < atom_counts[slot_ids // A_DEV]).astype(jnp.bfloat16)
    masked = features * alive_mask[:, None]
    source = jnp.dot(masked, source_weight, preferred_element_type=jnp.float32).astype(jnp.bfloat16)
    target = jnp.dot(masked, target_weight, preferred_element_type=jnp.float32).astype(jnp.bfloat16)
    charge = jnp.dot(masked, charge_weight, preferred_element_type=jnp.float32).astype(jnp.bfloat16)
    target_dom = target.reshape(domains, A_DEV, C)
    rows_dom = ghost_rows.reshape(4, domains, GHOST).transpose(1, 0, 2)
    outgoing = jax.vmap(lambda rows_table, picks: rows_table[picks])(target_dom, rows_dom)
    face_grid = outgoing.reshape(N_DX, N_DY, 4, GHOST, C)
    incoming = jnp.stack([jnp.roll(face_grid[:, :, 0], 1, 0), jnp.roll(face_grid[:, :, 1], -1, 0), jnp.roll(face_grid[:, :, 2], 1, 1), jnp.roll(face_grid[:, :, 3], -1, 1)], axis=2).reshape(domains, 4 * GHOST, C)
    target_table = jnp.concatenate([target_dom, incoming, jnp.zeros((domains, 1, C), jnp.bfloat16)], axis=1)
    source_dom = source.reshape(domains, A_DEV, C)
    neigh_dom = neighbours.reshape(domains, A_DEV, NB)
    dist_dom = distances.reshape(domains, A_DEV, NB)
    coord_dom = positions.reshape(3, domains, A_DEV).transpose(1, 0, 2)
    factor = wave_weights * (4.0 / math.sqrt(ATOMS * K))

    def forward_domain(block_items):
        return edge_forward(block_items[0], block_items[1], block_items[2], block_items[3], edge_weight)
    aggregate = lax.map(forward_domain, (source_dom, target_table, neigh_dom, dist_dom)).reshape(ATOMS, C)
    potential = ewald(charge.reshape(domains, A_DEV, CL), coord_dom, wavevectors, factor).reshape(ATOMS, CL)
    alive_wide = alive_mask.astype(jnp.float32)[:, None]
    layer_output = (alive_wide * (jnp.dot(aggregate, mix_weight, preferred_element_type=jnp.float32) + jnp.dot(potential, field_weight, preferred_element_type=jnp.float32))).astype(jnp.bfloat16)
    grad_masked = cotangent * alive_mask[:, None]
    grad_aggregate = contract_cols(grad_masked, mix_weight).astype(jnp.bfloat16)
    grad_potential = contract_cols(grad_masked, field_weight).astype(jnp.bfloat16)
    grad_charge = ewald(grad_potential.reshape(domains, A_DEV, CL), coord_dom, wavevectors, factor).reshape(ATOMS, CL)

    def backward_domain(running, block_items):
        edge_part, source_part, table_part = edge_backward(block_items[0], block_items[1], block_items[2], block_items[3], edge_weight, block_items[4])
        return (running + edge_part, (source_part, table_part))
    edge_sum, sums = lax.scan(backward_domain, jnp.zeros((C, C), jnp.float32), (source_dom, target_table, neigh_dom, dist_dom, grad_aggregate.reshape(domains, A_DEV, C)))
    source_sum, table_sum = sums
    ghost_grad = table_sum[:, A_DEV:A_DEV + 4 * GHOST].astype(jnp.bfloat16).reshape(N_DX, N_DY, 4, GHOST, C)
    returned = jnp.stack([jnp.roll(ghost_grad[:, :, 0], -1, 0), jnp.roll(ghost_grad[:, :, 1], 1, 0), jnp.roll(ghost_grad[:, :, 2], -1, 1), jnp.roll(ghost_grad[:, :, 3], 1, 1)], axis=2).reshape(domains, 4 * GHOST, C).astype(jnp.float32)
    target_sum = jax.vmap(lambda base_rows, picks, extra: base_rows.at[picks].add(extra))(table_sum[:, :A_DEV], rows_dom.reshape(domains, 4 * GHOST), returned)
    grad_source = source_sum.reshape(ATOMS, C).astype(jnp.bfloat16)
    grad_target = target_sum.reshape(ATOMS, C).astype(jnp.bfloat16)
    feature_grad = (alive_wide * (contract_cols(grad_source, source_weight) + contract_cols(grad_target, target_weight) + contract_cols(grad_charge, charge_weight))).astype(jnp.bfloat16)
    grad_scale = 1.0 / math.sqrt(ATOMS)
    return (layer_output, feature_grad, contract_rows(masked, grad_source) * grad_scale, contract_rows(masked, grad_target) * grad_scale, edge_sum * grad_scale, contract_rows(aggregate, grad_masked) * grad_scale, contract_rows(masked, grad_charge) * grad_scale, contract_rows(potential, grad_masked) * grad_scale)
```

```python
import math

import jax
import jax.numpy as jnp
from jax import lax
from jax.experimental import pallas as pl
from jax.experimental.pallas import tpu as pltpu
from jax.sharding import PartitionSpec as P

GEOMETRY = dict(y=8, z_hi=4, x=4, z_lo=2, core=2)
K = 2048
C = 128
A = 128
NB = 64
STEP = 8
COPIES = 100

BF = jnp.bfloat16
F32 = jnp.float32


def nn(a, b):
    return lax.dot_general(a, b, (((1,), (0,)), ((), ())), preferred_element_type=F32)


def nt(a, b):
    return lax.dot_general(a, b, (((1,), (1,)), ((), ())), preferred_element_type=F32)


def half_turns(f):
    q = f * f
    s = -0.007370430945714351
    for c in (
        0.08214588661112823,
        -0.5992645293207921,
        2.550164039877345,
        -5.16771278004997,
        3.141592653589793,
    ):
        s = s * q + c
    c0 = 0.0019295743094039231
    for c in (
        -0.02580689139001406,
        0.2353306303588935,
        -1.3352627688545893,
        4.058712126416768,
        -4.934802200544679,
        1.0,
    ):
        c0 = c0 * q + c
    return s * f, c0


def body(
    factor_scale,
    grad_scale,
    feat, pos, nbr, dist, ghost, counts, kvec, kw, sw, tw, ew, mw, cw, fw, cot,
    o_layer, o_feat, o_sg, o_tg, o_eg, o_mg, o_cg, o_fg,
    cs, part, full, rc, b1, rx, b2, ry, b3, rz,
    gout, gin, ggout, gret,
    g0, rgx, g1, rgy, g2, rgz, gfull,
    h0, rhy, h1, rhz, h2, rhx, hfull,
    nbr_t, gate_t, src_t, ga_t, tab_t, pick_t, agg_t, gs_t, tsum, epart,
    ssem, rsem,
):
    geo = GEOMETRY
    nx, ny, nc = geo["x"], geo["y"], geo["core"]
    nzl, nzh = geo["z_lo"], geo["z_hi"]
    nz = nzl * nzh
    ndx, ndy = ny * nzh * nx, nzl * nc
    dx, dy = lax.axis_index("dx"), lax.axis_index("dy")
    x = lax.rem(dx, nx)
    zh = lax.rem(lax.div(dx, nx), nzh)
    y = lax.div(dx, nx * nzh)
    zl, core = lax.div(dy, nc), lax.rem(dy, nc)
    z = zh * nzl + zl

    def device(px=None, py=None, pz=None, pc=None):
        px = x if px is None else px
        py = y if py is None else py
        pz = z if pz is None else pz
        pc = core if pc is None else pc
        return (
            (py * nzh + lax.div(pz, nzl)) * nx + px,
            lax.rem(pz, nzl) * nc + pc,
        )

    def ahead(me, d, n):
        return lax.rem(me + d, n)

    def x_peer(d):
        return device(px=ahead(x, d, nx))

    def y_peer(d):
        return device(py=ahead(y, d, ny))

    def z_peer(d):
        return device(pz=ahead(z, d, nz))

    def zc_peer(d):
        return device(pz=ahead(z, d // nc, nz), pc=ahead(core, d % nc, nc))

    def xc_peer(d):
        return device(px=ahead(x, d // nc, nx), pc=ahead(core, d % nc, nc))

    sibling = device(pc=ahead(core, 1, nc))
    faces = (
        (ahead(dx, 1, ndx), dy),
        (ahead(dx, ndx - 1, ndx), dy),
        (dx, ahead(dy, 1, ndy)),
        (dx, ahead(dy, ndy - 1, ndy)),
    )
    back = (faces[1], faces[0], faces[3], faces[2])

    barrier = pltpu.get_barrier_semaphore()
    greeted = list(faces)
    greeted += [y_peer(d) for d in range(1, ny)]
    greeted += [zc_peer(d) for d in range(1, nz * nc)]
    greeted += [xc_peer(d) for d in range(1, nx * nc) if d // nc]
    for other in greeted:
        pl.semaphore_signal(
            barrier, inc=1, device_id=other, device_id_type=pl.DeviceIdType.MESH
        )

    sent = []

    def send(src, dst, other):
        slot = len(sent)
        copy = pltpu.make_async_remote_copy(
            src_ref=src,
            dst_ref=dst,
            send_sem=ssem.at[slot],
            recv_sem=rsem.at[slot],
            device_id=other,
            device_id_type=pl.DeviceIdType.MESH,
        )
        copy.start()
        sent.append(copy)
        return copy

    def arrive(copies):
        for copy in copies:
            copy.wait_recv()

    def rows(ref, start, size):
        return ref.at[pl.ds(pl.multiple_of(start, 16), size)]

    def scatter(src, landing, me, n, size, peer):
        return [
            send(rows(src, ahead(me, d, n) * size, size), landing.at[d - 1], peer(d))
            for d in range(1, n)
        ]

    def collect(src, landing, me, n, size, dst):
        chunk = min(size, 128)

        def add(i, _):
            at = pl.multiple_of(i * chunk, 16)
            total = src[pl.ds(pl.multiple_of(me * size + at, 16), chunk), :].astype(F32)
            for d in range(1, n):
                total += landing[d - 1, pl.ds(at, chunk), :].astype(F32)
            dst[pl.ds(at, chunk), :] = total.astype(BF)
            return 0

        lax.fori_loop(0, size // chunk, add, 0)

    def share(landing, me, n, peer):
        return [send(landing.at[me], landing.at[me], peer(d)) for d in range(1, n)]

    def summed_slots(landing, n):
        total = landing[0].astype(F32)
        for d in range(1, n):
            total += landing[d].astype(F32)
        return total.astype(BF)

    def spread(ref, start, size, n, peer):
        return [
            send(rows(ref, start, size), rows(ref, start, size), peer(d)) for d in range(1, n)
        ]

    row_id = lax.broadcasted_iota(jnp.int32, (A, C), 0)
    alive = jnp.where(row_id < counts[0], 1.0, 0.0).astype(F32)
    masked32 = feat[...].astype(F32) * alive
    gm32 = cot[...].astype(F32) * alive
    masked, gm = masked32.astype(BF), gm32.astype(BF)
    masked_t = masked32.T.astype(BF)
    target = nn(masked, tw[...]).astype(BF)
    for f in range(4):
        pick_t[:, f * 32 : (f + 1) * 32] = jnp.where(
            lax.broadcasted_iota(jnp.int32, (A, 32), 0) == ghost[f : f + 1, :], 1.0, 0.0
        )
    pick = pick_t[...].T.astype(BF)
    gout[...] = nn(pick, target).astype(BF)

    pl.semaphore_wait(barrier, len(greeted))
    ghosts_in = [
        send(gout.at[pl.ds(f * 32, 32)], gin.at[pl.ds(f * 32, 32)], faces[f]) for f in range(4)
    ]

    cw_t = cw[...].astype(F32).T.astype(BF)
    values_t = jnp.concatenate([nt(cw_t, masked), nt(fw[...], gm)], axis=0).astype(BF)
    columns = [jnp.broadcast_to(pos[a : a + 1, :], (A, A)).T for a in range(3)]
    turn = 1.0 / (2.0 * math.pi)
    for block in range(K // 128):
        at = slice(block * 128, (block + 1) * 128)
        turns = (
            columns[0] * (kvec[0:1, at] * turn)
            + columns[1] * (kvec[1:2, at] * turn)
            + columns[2] * (kvec[2:3, at] * turn)
        )
        turns = turns - jnp.floor(turns + 0.5)
        s, c = half_turns(turns)
        cosine = (1.0 - 2.0 * s * s).astype(BF)
        sine = (2.0 * s * c).astype(BF)
        cs[:, at] = cosine
        cs[:, K + block * 128 : K + (block + 1) * 128] = sine
        part[block * 128 : (block + 1) * 128, :] = nn(values_t, cosine).astype(BF)
        part[K + block * 128 : K + (block + 1) * 128, :] = nn(values_t, sine).astype(BF)

    half = 2 * K // nc
    to_sibling = scatter(part, rc, core, nc, half, lambda d: sibling)

    src_t[...] = nn(masked, sw[...]).astype(BF).astype(F32).T
    ga_t[...] = nt(gm, mw[...]).astype(BF).astype(F32).T
    nbr_t[...] = nbr[...].astype(F32).T
    s, c = half_turns(dist[...] * 0.1)
    gate_t[...] = jnp.where(nbr[...] < 2 * A, c * c, 0.0).T
    tab_t[:, :A] = target.astype(F32).T.astype(BF)
    agg_t[...] = jnp.zeros_like(agg_t)
    gs_t[...] = jnp.zeros_like(gs_t)
    tsum[...] = jnp.zeros_like(tsum)
    epart[...] = jnp.zeros_like(epart)

    arrive(to_sibling)
    collect(part, rc, core, nc, half, b1)
    quarter = half // nx
    x_scatter = scatter(b1, rx, x, nx, quarter, x_peer)

    arrive(ghosts_in)
    tab_t[:, A:] = gin[...].astype(F32).T.astype(BF)

    ew_t = ew[...].astype(F32).T.astype(BF)

    def edge_step(step, _):
        table_row = lax.broadcasted_iota(jnp.int32, (2 * A, A), 0).astype(F32)
        hiddens, inners, picks, pairs = [], [], [], []
        agg_sum, gs_sum = agg_t[...], gs_t[...]
        source, upstream = src_t[...], ga_t[...]
        for pair in range(STEP // 2):
            base = step * STEP + 2 * pair
            gates = [gate_t[pl.ds(base + j, 1), :] for j in range(2)]
            chosen = jnp.concatenate(
                [
                    jnp.where(table_row == nbr_t[pl.ds(base + j, 1), :], 1.0, 0.0).astype(BF)
                    for j in range(2)
                ],
                axis=1,
            )
            summed = nn(tab_t[...], chosen) + jnp.concatenate([source, source], axis=1)
            g = 0.5 * jnp.tanh(0.5 * summed) + 0.5
            hidden = summed * g
            slope = g + hidden * (1.0 - g)
            hidden = hidden.astype(BF)
            mixed = nn(ew_t, hidden)
            g = 0.5 * jnp.tanh(0.5 * mixed) + 0.5
            message = mixed * g
            mixed_slope = g + message * (1.0 - g)
            agg_sum += gates[0] * message[:, :A] + gates[1] * message[:, A:]
            inner = jnp.concatenate(
                [
                    gates[0] * upstream * mixed_slope[:, :A],
                    gates[1] * upstream * mixed_slope[:, A:],
                ],
                axis=1,
            ).astype(BF)
            pair_grad = nn(ew[...], inner) * slope
            gs_sum += pair_grad[:, :A] + pair_grad[:, A:]
            hiddens.append(hidden)
            inners.append(inner)
            picks.append(chosen)
            pairs.append(pair_grad.astype(BF))
        agg_t[...] = agg_sum
        gs_t[...] = gs_sum
        epart[...] += nt(jnp.concatenate(hiddens, axis=1), jnp.concatenate(inners, axis=1))
        tsum[...] += nt(jnp.concatenate(picks, axis=1), jnp.concatenate(pairs, axis=1))
        return 0

    lax.fori_loop(0, NB // STEP, edge_step, 0)

    ggout[...] = tsum[A:, :].astype(BF)
    ghosts_back = [
        send(ggout.at[pl.ds(f * 32, 32)], gret.at[pl.ds(f * 32, 32)], back[f]) for f in range(4)
    ]

    arrive(x_scatter)
    collect(b1, rx, x, nx, quarter, b2)
    piece = quarter // ny
    y_scatter = scatter(b2, ry, y, ny, piece, y_peer)

    aggregate_t = agg_t[...].astype(BF)
    aggregate = agg_t[...].T.astype(BF)
    grad_source = gs_t[...].T.astype(BF)
    short_range = nn(aggregate, mw[...])
    g0[0:C, :] = nn(masked_t, grad_source).astype(BF)
    g0[2 * C : 3 * C, :] = epart[...].astype(BF)
    g0[3 * C :, :] = nn(aggregate_t, gm).astype(BF)
    arrive(ghosts_back)
    grad_target = (tsum[:A, :] + nn(pick_t[...].astype(BF), gret[...])).astype(BF)
    g0[C : 2 * C, :] = nn(masked_t, grad_target).astype(BF)
    gx, gy = 4 * C // nx, 4 * C // (nx * ny)
    g_x = scatter(g0, rgx, x, nx, gx, x_peer)
    short_grad = nt(grad_source, sw[...]) + nt(grad_target, tw[...])

    arrive(y_scatter)
    collect(b2, ry, y, ny, piece, b3)
    rz[pl.ds(z, 1)] = b3[...][None]
    z_share = share(rz, z, nz, z_peer)

    arrive(g_x)
    collect(g0, rgx, x, nx, gx, g1)
    g_y = scatter(g1, rgy, y, ny, gy, y_peer)

    arrive(z_share)
    mine = pl.multiple_of(core * half + x * quarter + y * piece, 16)
    full[pl.ds(mine, piece), :] = summed_slots(rz, nz)
    y_spread = spread(full, mine, piece, ny, y_peer)

    arrive(g_y)
    collect(g1, rgy, y, ny, gy, g2)
    zc = z * nc + core
    rgz[pl.ds(zc, 1)] = g2[...][None]
    g_zc = share(rgz, zc, nz * nc, zc_peer)

    arrive(y_spread)
    x_spread = spread(full, core * half + x * quarter, quarter, nx, x_peer)

    arrive(g_zc)
    g_mine = pl.multiple_of(x * gx + y * gy, 16)
    gfull[pl.ds(g_mine, gy), :] = summed_slots(rgz, nz * nc)
    g_ys = spread(gfull, g_mine, gy, ny, y_peer)

    arrive(x_spread)
    c_spread = spread(full, core * half, half, nc, lambda d: sibling)

    arrive(g_ys)
    g_xs = spread(gfull, x * gx, gx, nx, x_peer)

    arrive(c_spread)
    field = jnp.zeros((A, C), F32)
    for block in range(2 * K // 256):
        at = [slice(block * 256 + j * 128, block * 256 + (j + 1) * 128) for j in range(2)]
        factors = [
            kw[:, (a.start % K) : (a.start % K) + 128] * factor_scale for a in at
        ]
        weights = jnp.concatenate(
            [(full[a, :].astype(F32) * w).astype(BF) for a, w in zip(at, factors)], axis=1
        )
        field += nt(cs[:, block * 256 : (block + 1) * 256], weights)
    field = field.astype(BF).astype(F32)
    potential = field[:, :64].astype(BF)
    grad_charge = field[:, 64:].astype(BF)
    field_t = field.T.astype(BF)
    h0[:64, :] = nn(field_t[64:, :], masked).astype(BF)
    h0[64:, :] = nn(field_t[:64, :], gm).astype(BF)
    hy = C // ny
    h_y = scatter(h0, rhy, y, ny, hy, y_peer)

    o_layer[...] = (alive * (short_range + nn(potential, fw[...]))).astype(BF)
    o_feat[...] = (alive * (short_grad + nt(grad_charge, cw[...]))).astype(BF)
    arrive(g_xs)
    for i, out in enumerate((o_sg, o_tg, o_eg, o_mg)):
        out[...] = gfull[i * C : (i + 1) * C, :].astype(F32) * grad_scale

    arrive(h_y)
    collect(h0, rhy, y, ny, hy, h1)
    rhz[pl.ds(z, 1)] = h1[...][None]
    h_z = share(rhz, z, nz, z_peer)
    arrive(h_z)
    h2[...] = summed_slots(rhz, nz)
    xc = x * nc + core
    rhx[pl.ds(xc, 1)] = h2[...][None]
    h_x = share(rhx, xc, nx * nc, xc_peer)
    arrive(h_x)
    h_mine = pl.multiple_of(y * hy, 16)
    hfull[pl.ds(h_mine, hy), :] = summed_slots(rhx, nx * nc)
    arrive(spread(hfull, h_mine, hy, ny, y_peer))
    o_cg[...] = (hfull[:64, :].astype(F32) * grad_scale).T
    o_fg[...] = hfull[64:, :].astype(F32) * grad_scale

    for copy in sent:
        copy.wait_send()


def local(
    features, positions, neighbours, distances, ghost_rows, atom_counts, wavevectors,
    wave_weights, source_weight, target_weight, edge_weight, mix_weight, charge_weight,
    field_weight, cotangent,
):
    geo = GEOMETRY
    nx, ny, nc, nz = geo["x"], geo["y"], geo["core"], geo["z_lo"] * geo["z_hi"]
    total_atoms = A * lax.axis_size("dx") * lax.axis_size("dy")
    factor_scale = 4.0 / math.sqrt(total_atoms * K)
    grad_scale = 1.0 / math.sqrt(total_atoms)
    half = 2 * K // nc
    quarter = half // nx
    piece = quarter // ny
    gx, gy, hy = 4 * C // nx, 4 * C // (nx * ny), C // ny

    def bf(*shape):
        return pltpu.VMEM(shape, BF)

    def f32(*shape):
        return pltpu.VMEM(shape, F32)

    scratch = [
        bf(A, 2 * K), bf(2 * K, C), bf(2 * K, C),
        bf(nc - 1, half, C), bf(half, C),
        bf(nx - 1, quarter, C), bf(quarter, C),
        bf(ny - 1, piece, C), bf(piece, C),
        bf(nz, piece, C),
        bf(A, C), bf(A, C), bf(A, C), bf(A, C),
        bf(4 * C, C), bf(nx - 1, gx, C), bf(gx, C), bf(ny - 1, gy, C), bf(gy, C),
        bf(nz * nc, gy, C), bf(4 * C, C),
        bf(C, C), bf(ny - 1, hy, C), bf(hy, C), bf(nz, hy, C), bf(hy, C),
        bf(nx * nc, hy, C), bf(C, C),
        f32(NB, A), f32(NB, A), f32(C, A), f32(C, A), bf(C, 2 * A), f32(A, A),
        f32(C, A), f32(C, A), f32(2 * A, C), f32(C, C),
        pltpu.SemaphoreType.DMA((COPIES,)),
        pltpu.SemaphoreType.DMA((COPIES,)),
    ]
    vmem = pl.BlockSpec(memory_space=pltpu.VMEM)
    specs = [vmem] * 15
    specs[5] = pl.BlockSpec(memory_space=pltpu.SMEM)
    outs = [
        jax.ShapeDtypeStruct((A, C), BF),
        jax.ShapeDtypeStruct((A, C), BF),
        jax.ShapeDtypeStruct((C, C), F32),
        jax.ShapeDtypeStruct((C, C), F32),
        jax.ShapeDtypeStruct((C, C), F32),
        jax.ShapeDtypeStruct((C, C), F32),
        jax.ShapeDtypeStruct((C, 64), F32),
        jax.ShapeDtypeStruct((64, C), F32),
    ]

    def kernel(*refs):
        body(factor_scale, grad_scale, *refs)

    return pl.pallas_call(
        kernel,
        out_shape=outs,
        in_specs=specs,
        out_specs=[vmem] * 8,
        scratch_shapes=scratch,
        compiler_params=pltpu.CompilerParams(
            collective_id=0, has_side_effects=True, vmem_limit_bytes=40 * 1024 * 1024
        ),
        name="ewald_layer",
    )(
        features, positions, neighbours, distances, ghost_rows, atom_counts, wavevectors,
        wave_weights.reshape(1, K), source_weight, target_weight, edge_weight, mix_weight,
        charge_weight, field_weight, cotangent,
    )


def solution(mesh):
    atoms = P(("dx", "dy"), None)
    in_specs = (
        atoms, P(None, ("dx", "dy")), atoms, atoms, P(None, ("dx", "dy")), P(("dx", "dy")),
        P(), P(), P(), P(), P(), P(), P(), P(), atoms,
    )
    out_specs = (atoms, atoms, P(), P(), P(), P(), P(), P())
    return jax.shard_map(
        local, mesh=mesh, in_specs=in_specs, out_specs=out_specs, check_vma=False
    )
```

```python
import math

import jax
import jax.numpy as jnp
from jax import lax
from jax.experimental import pallas as pl
from jax.experimental.pallas import tpu as pltpu
from jax.sharding import PartitionSpec as P

GEOMETRY = dict(y=8, z_hi=4, x=4, z_lo=2, core=2)
K = 2048
C = 128
A = 128
NB = 64
STEP = 8
COPIES = 140
ROWS = (1024, 512, 512)

FIRST = (0, 14, 4, 5, 1)
LATER = (6, 7, 2, 3, 8, 9, 10, 11, 12, 13)

BF = jnp.bfloat16
F32 = jnp.float32


def nn(a, b):
    return lax.dot_general(a, b, (((1,), (0,)), ((), ())), preferred_element_type=F32)


def nt(a, b):
    return lax.dot_general(a, b, (((1,), (1,)), ((), ())), preferred_element_type=F32)


def half_turns(f):
    q = f * f
    s = -0.007370430945714351
    for c in (
        0.08214588661112823,
        -0.5992645293207921,
        2.550164039877345,
        -5.16771278004997,
        3.141592653589793,
    ):
        s = s * q + c
    c0 = 0.0019295743094039231
    for c in (
        -0.02580689139001406,
        0.2353306303588935,
        -1.3352627688545893,
        4.058712126416768,
        -4.934802200544679,
        1.0,
    ):
        c0 = c0 * q + c
    return s * f, c0


def body(
    factor_scale,
    grad_scale,
    operands,
    out,
    held, held_sem,
    x_out, x_in, pos_out, pos_in, kv, sums,
    la, ta, lb, tb, lc, tc, la2, lb2, lc2, t2, lz, ly, fin,
    w_out, w_in, w_full, cosine, sine, e_out, e_in,
    gout, gin, ggout, gret,
    g0, rgx, g1, rgy, g2, rgz, gfull,
    rhy, rhz, rhx, h2, h_in,
    nbr_t, gate_t, src_t, ga_t, tab_t, pick_t, agg_t, gs_t, tsum, epart,
    ssem, rsem,
):
    fetch = [
        pltpu.make_async_copy(src, dst, held_sem.at[i])
        for i, (src, dst) in enumerate(zip(operands, held))
    ]
    for i in FIRST + LATER:
        fetch[i].start()
    feat, pos, nbr, dist, ghost, counts, kvec, kw, sw, tw, ew, mw, cw, fw, cot = held

    geo = GEOMETRY
    nx, ny, nc = geo["x"], geo["y"], geo["core"]
    nzl, nzh = geo["z_lo"], geo["z_hi"]
    nz = nzl * nzh
    ndx, ndy = ny * nzh * nx, nzl * nc
    dx, dy = lax.axis_index("dx"), lax.axis_index("dy")
    x = lax.rem(dx, nx)
    zh = lax.rem(lax.div(dx, nx), nzh)
    y = lax.div(dx, nx * nzh)
    zl, core = lax.div(dy, nc), lax.rem(dy, nc)
    z = zh * nzl + zl

    def device(px=None, py=None, pz=None, pc=None):
        px = x if px is None else px
        py = y if py is None else py
        pz = z if pz is None else pz
        pc = core if pc is None else pc
        return (
            (py * nzh + lax.div(pz, nzl)) * nx + px,
            lax.rem(pz, nzl) * nc + pc,
        )

    def ahead(me, d, n):
        return lax.rem(me + d, n)

    def x_peer(d):
        return device(px=ahead(x, d, nx))

    def y_peer(d):
        return device(py=ahead(y, d, ny))

    def z_peer(d):
        return device(pz=ahead(z, d, nz))

    def zc_peer(d):
        return device(pz=ahead(z, d // nc, nz), pc=ahead(core, d % nc, nc))

    sibling = device(pc=ahead(core, 1, nc))
    faces = (
        (ahead(dx, 1, ndx), dy),
        (ahead(dx, ndx - 1, ndx), dy),
        (dx, ahead(dy, 1, ndy)),
        (dx, ahead(dy, ndy - 1, ndy)),
    )
    back = (faces[1], faces[0], faces[3], faces[2])

    barrier = pltpu.get_barrier_semaphore()
    greeted = list(faces)
    greeted += [x_peer(d) for d in range(1, nx)]
    greeted += [y_peer(d) for d in range(1, ny)]
    greeted += [zc_peer(d) for d in range(1, nz * nc)]
    for other in greeted:
        pl.semaphore_signal(
            barrier, inc=1, device_id=other, device_id_type=pl.DeviceIdType.MESH
        )

    sent = []

    def send(src, dst, other):
        slot = len(sent)
        copy = pltpu.make_async_remote_copy(
            src_ref=src,
            dst_ref=dst,
            send_sem=ssem.at[slot],
            recv_sem=rsem.at[slot],
            device_id=other,
            device_id_type=pl.DeviceIdType.MESH,
        )
        copy.start()
        sent.append(copy)
        return copy

    def arrive(copies):
        for copy in copies:
            copy.wait_recv()

    def rows(ref, start, size):
        return ref.at[pl.ds(pl.multiple_of(start, 16), size)]

    def scatter(src, base, landing, me, n, size, peer):
        return [
            send(rows(src, base + ahead(me, d, n) * size, size), landing.at[d - 1], peer(d))
            for d in range(1, n)
        ]

    def collect(src, base, landing, me, n, size, dst, dst_base=0):
        chunk = min(size, 128)

        def add(i, _):
            at = pl.multiple_of(i * chunk, 16)
            total = src[pl.ds(pl.multiple_of(base + me * size + at, 16), chunk), :].astype(F32)
            for d in range(1, n):
                total += landing[d - 1, pl.ds(at, chunk), :].astype(F32)
            dst[pl.ds(pl.multiple_of(dst_base + at, 16), chunk), :] = total.astype(BF)
            return 0

        if size == chunk:
            add(0, 0)
        else:
            lax.fori_loop(0, size // chunk, add, 0)

    def share(landing, me, n, peer):
        return [send(landing.at[me], landing.at[me], peer(d)) for d in range(1, n)]

    def summed_slots(landing, n):
        total = landing[0].astype(F32)
        for d in range(1, n):
            total += landing[d].astype(F32)
        return total

    def spread(ref, start, size, n, peer):
        return [
            send(rows(ref, start, size), rows(ref, start, size), peer(d)) for d in range(1, n)
        ]

    first_core = jnp.where(core == 0, 1.0, 0.0).astype(F32)

    def by_core(mine_if_first, mine_if_second):
        return first_core * mine_if_first + (1.0 - first_core) * mine_if_second

    for i in FIRST:
        fetch[i].wait()

    row_id = lax.broadcasted_iota(jnp.int32, (A, C), 0)
    alive = jnp.where(row_id < counts[0], 1.0, 0.0).astype(F32)
    masked32 = feat[...].astype(F32) * alive
    gm32 = cot[...].astype(F32) * alive
    masked, gm = masked32.astype(BF), gm32.astype(BF)
    for f in range(4):
        pick_t[:, f * 32 : (f + 1) * 32] = jnp.where(
            lax.broadcasted_iota(jnp.int32, (A, 32), 0) == ghost[f : f + 1, :], 1.0, 0.0
        )
    gout[...] = nn(pick_t[...].T.astype(BF), masked).astype(BF)
    x_out[...] = by_core(gm32, masked32).astype(BF)
    pos_out[...] = jnp.zeros_like(pos_out)
    pos_out[0:3, :] = pos[...]

    pl.semaphore_wait(barrier, len(greeted))
    atoms_in = [send(x_out, x_in, sibling), send(pos_out, pos_in, sibling)]
    ghosts_in = [
        send(gout.at[pl.ds(f * 32, 32)], gin.at[pl.ds(f * 32, 32)], faces[f]) for f in range(4)
    ]

    for i in LATER:
        fetch[i].wait()

    masked_t = masked32.T.astype(BF)
    kv[...] = jnp.zeros_like(kv)
    kv[0:3, :] = kvec[...] * (1.0 / (2.0 * math.pi))
    kv[3:4, :] = jnp.sqrt(kw[...] * factor_scale)
    own_kind = by_core(masked32, gm32).astype(BF)

    src_t[...] = nn(masked, sw[...]).astype(BF).astype(F32).T
    ga_t[...] = nt(gm, mw[...]).astype(BF).astype(F32).T
    nbr_t[...] = nbr[...].astype(F32)
    s, c = half_turns(dist[...] * 0.1)
    gate_t[...] = jnp.where(nbr[...] < 2 * A, c * c, 0.0)
    tab_t[:, :A] = nn(masked, tw[...]).astype(BF).astype(F32).T.astype(BF)
    agg_t[...] = jnp.zeros_like(agg_t)
    gs_t[...] = jnp.zeros_like(gs_t)
    tsum[...] = jnp.zeros_like(tsum)
    epart[...] = jnp.zeros_like(epart)
    ew_t = ew[...].astype(F32).T.astype(BF)

    arrive(atoms_in)
    both = jnp.concatenate([own_kind, x_in[...]], axis=0)
    spots = [
        jnp.concatenate([pos[a : a + 1, :], pos_in[a : a + 1, :]], axis=1) for a in range(3)
    ]

    def waves(turns, root):
        turns = turns - jnp.floor(turns + 0.5)
        s, c = half_turns(turns)
        return ((1.0 - 2.0 * s * s) * root).astype(BF), ((2.0 * s * c) * root).astype(BF)

    def sum_block(block, _):
        at = pl.multiple_of(block * 128, 128)
        cols = kv[:, pl.ds(at, 128)].T
        turns = cols[:, 0:1] * spots[0] + cols[:, 1:2] * spots[1] + cols[:, 2:3] * spots[2]
        cos_t, sin_t = waves(turns, cols[:, 3:4])
        sums[pl.ds(at, 128), :C] = nn(cos_t, both).astype(BF)
        sums[pl.ds(at, 128), C:] = nn(sin_t, both).astype(BF)
        return 0

    base_a, base_b, base_c = 0, ROWS[0], ROWS[0] + ROWS[1]
    a1, b1, c1 = ROWS[0] // nx, ROWS[1] // ny, ROWS[2] // nz
    a2, b2, c2 = a1 // ny, b1 // nx, c1 // nx
    lax.fori_loop(0, base_b // 128, sum_block, 0)
    first_a = scatter(sums, base_a, la, x, nx, a1, x_peer)
    lax.fori_loop(base_b // 128, base_c // 128, sum_block, 0)
    first_b = scatter(sums, base_b, lb, y, ny, b1, y_peer)
    lax.fori_loop(base_c // 128, K // 128, sum_block, 0)
    first_c = scatter(sums, base_c, lc, z, nz, c1, z_peer)

    arrive(ghosts_in)
    ghosts = gin[...]
    tab_t[:, A:] = nn(ghosts, tw[...]).astype(BF).astype(F32).T.astype(BF)
    table_t = jnp.concatenate([masked_t, ghosts.astype(F32).T.astype(BF)], axis=1)
    def edge_step(step, _):
        table_row = lax.broadcasted_iota(jnp.int32, (2 * A, A), 0).astype(F32)
        hiddens, inners, picks, pairs = [], [], [], []
        agg_sum, gs_sum = agg_t[...], gs_t[...]
        source, upstream = src_t[...], ga_t[...]
        for pair in range(STEP // 2):
            base = step * STEP + 2 * pair
            gates = [gate_t[pl.ds(base + j, 1), :] for j in range(2)]
            chosen = jnp.concatenate(
                [
                    jnp.where(table_row == nbr_t[pl.ds(base + j, 1), :], 1.0, 0.0).astype(BF)
                    for j in range(2)
                ],
                axis=1,
            )
            summed = nn(tab_t[...], chosen) + jnp.concatenate([source, source], axis=1)
            g = 0.5 * jnp.tanh(0.5 * summed) + 0.5
            hidden = summed * g
            slope = g + hidden * (1.0 - g)
            hidden = hidden.astype(BF)
            mixed = nn(ew_t, hidden)
            g = 0.5 * jnp.tanh(0.5 * mixed) + 0.5
            message = mixed * g
            mixed_slope = g + message * (1.0 - g)
            agg_sum += gates[0] * message[:, :A] + gates[1] * message[:, A:]
            inner = jnp.concatenate(
                [
                    gates[0] * upstream * mixed_slope[:, :A],
                    gates[1] * upstream * mixed_slope[:, A:],
                ],
                axis=1,
            ).astype(BF)
            pair_grad = nn(ew[...], inner) * slope
            gs_sum += pair_grad[:, :A] + pair_grad[:, A:]
            hiddens.append(hidden)
            inners.append(inner)
            picks.append(chosen)
            pairs.append(pair_grad.astype(BF))
        agg_t[...] = agg_sum
        gs_t[...] = gs_sum
        epart[...] += nt(jnp.concatenate(hiddens, axis=1), jnp.concatenate(inners, axis=1))
        tsum[...] += nt(jnp.concatenate(picks, axis=1), jnp.concatenate(pairs, axis=1))
        return 0

    steps = NB // STEP
    cut = (steps // 2, steps - 1)
    lax.fori_loop(0, cut[0], edge_step, 0)
    arrive(first_a)
    collect(sums, base_a, la, x, nx, a1, ta)
    second_a = scatter(ta, 0, la2, y, ny, a2, y_peer)
    arrive(first_b)
    collect(sums, base_b, lb, y, ny, b1, tb)
    second_b = scatter(tb, 0, lb2, x, nx, b2, x_peer)
    arrive(first_c)
    collect(sums, base_c, lc, z, nz, c1, tc)
    second_c = scatter(tc, 0, lc2, x, nx, c2, x_peer)

    lax.fori_loop(cut[0], cut[1], edge_step, 0)
    ab2 = a2 + b2
    arrive(second_b)
    collect(tb, 0, lb2, x, nx, b2, t2, a2)
    arrive(second_c)
    collect(tc, 0, lc2, x, nx, c2, t2, ab2)
    ly[pl.ds(y, 1)] = t2[ab2:, :][None]
    third_c = share(ly, y, ny, y_peer)
    arrive(second_a)
    collect(ta, 0, la2, y, ny, a2, t2, 0)
    lz[pl.ds(z, 1)] = t2[:ab2, :][None]
    third_ab = share(lz, z, nz, z_peer)

    lax.fori_loop(cut[1], steps, edge_step, 0)

    table_sum = tsum[...]
    ggout[...] = table_sum[A:, :].astype(BF)
    ghosts_back = [
        send(ggout.at[pl.ds(f * 32, 32)], gret.at[pl.ds(f * 32, 32)], back[f]) for f in range(4)
    ]
    aggregate_t = agg_t[...].astype(BF)
    grad_source = gs_t[...].T.astype(BF)
    g0[0:C, :] = nn(masked_t, grad_source).astype(BF)
    g0[C : 2 * C, :] = nn(table_t, table_sum.astype(BF)).astype(BF)
    g0[2 * C : 3 * C, :] = epart[...].astype(BF)
    g0[3 * C :, :] = nn(aggregate_t, gm).astype(BF)
    gx, gy = 4 * C // nx, 4 * C // (nx * ny)
    g_x = scatter(g0, 0, rgx, x, nx, gx, x_peer)

    fw_t = fw[...].astype(F32).T
    project = by_core(cw[...].astype(F32).T, fw_t).astype(BF)
    none = jnp.zeros((C, 64), BF)
    project = jnp.concatenate(
        [
            jnp.concatenate([project, none], axis=1),
            jnp.concatenate([none, project], axis=1),
        ],
        axis=0,
    )
    arrive(third_c)
    fin[ab2:, :] = summed_slots(ly, ny).astype(BF)
    arrive(third_ab)
    fin[:ab2, :] = summed_slots(lz, nz).astype(BF)
    w_out[...] = nn(fin[...], project).astype(BF)
    place_a = pl.multiple_of(base_a + x * a1 + y * a2, 16)
    place_b = pl.multiple_of(base_b + y * b1 + x * b2, 16)
    place_c = pl.multiple_of(base_c + z * c1 + x * c2, 16)
    w_full[pl.ds(place_a, a2), :] = w_out[:a2, :]
    w_full[pl.ds(place_b, b2), :] = w_out[a2:ab2, :]
    w_full[pl.ds(place_c, c2), :] = w_out[ab2:, :]
    spread_a = spread(w_full, place_a, a2, ny, y_peer)
    spread_b = spread(w_full, place_b, b2, nx, x_peer)
    spread_c = spread(w_full, place_c, c2, nx, x_peer)
    w_swap = [send(w_out, w_in, sibling)]

    arrive(g_x)
    collect(g0, 0, rgx, x, nx, gx, g1)
    g_y = scatter(g1, 0, rgy, y, ny, gy, y_peer)

    arrive(w_swap)
    other_t = w_in[...].astype(F32).T
    in_ab = lax.broadcasted_iota(jnp.int32, other_t.shape, 1) < ab2

    def weight_part(left):
        quads = nn(left.astype(BF), fin[...])
        return (quads[:64, :C] + quads[64:, C:]).astype(BF)

    rhy[pl.ds(y, 1)] = weight_part(jnp.where(in_ab, other_t, 0.0))[None]
    rhz[pl.ds(z, 1)] = weight_part(jnp.where(in_ab, 0.0, other_t))[None]

    arrive(spread_b)
    spread_b = spread(w_full, base_b + y * b1, b1, ny, y_peer)
    arrive(spread_c)
    spread_c = spread(w_full, base_c + z * c1, c1, nz, z_peer)
    h_y = share(rhy, y, ny, y_peer)
    h_z = share(rhz, z, nz, z_peer)
    arrive(spread_a)
    spread_a = spread(w_full, base_a + x * a1, a1, nx, x_peer)

    spot_cols = [
        jnp.concatenate(
            [
                jnp.broadcast_to(pos[a : a + 1, :], (A, A)).T,
                jnp.broadcast_to(pos_in[a : a + 1, :], (A, A)).T,
            ],
            axis=0,
        )
        for a in range(3)
    ]

    def wave_block(block, _):
        at = pl.ds(pl.multiple_of(block * 128, 128), 128)
        turns = (
            spot_cols[0] * kv[0:1, at] + spot_cols[1] * kv[1:2, at] + spot_cols[2] * kv[2:3, at]
        )
        cosine[:, at], sine[:, at] = waves(turns, kv[3:4, at])
        return 0

    lax.fori_loop(0, K // 128, wave_block, 0)

    arrive(g_y)
    collect(g1, 0, rgy, y, ny, gy, g2)
    zc = z * nc + core
    rgz[pl.ds(zc, 1)] = g2[...][None]
    g_zc = share(rgz, zc, nz * nc, zc_peer)

    arrive(ghosts_back)
    grad_target = (table_sum[:A, :] + nn(pick_t[...].astype(BF), gret[...])).astype(BF)
    short_grad = nt(grad_source, sw[...]) + nt(grad_target, tw[...])
    short_range = nn(agg_t[...].T.astype(BF), mw[...])

    arrive(h_y)
    arrive(h_z)
    rhx[pl.ds(x, 1)] = (summed_slots(rhy, ny) + summed_slots(rhz, nz)).astype(BF)[None]
    h_x = share(rhx, x, nx, x_peer)

    arrive(spread_b)
    arrive(spread_c)
    arrive(spread_a)
    field = nn(cosine[...], w_full[...]) + pltpu.roll(nn(sine[...], w_full[...]), 64, 1)
    e_out[...] = field[A:, :].astype(BF)
    e_swap = [send(e_out, e_in, sibling)]

    arrive(g_zc)
    g_mine = pl.multiple_of(x * gx + y * gy, 16)
    gfull[pl.ds(g_mine, gy), :] = summed_slots(rgz, nz * nc).astype(BF)
    g_ys = spread(gfull, g_mine, gy, ny, y_peer)

    arrive(h_x)
    h2[...] = summed_slots(rhx, nx).astype(BF)
    h_swap = [send(h2, h_in, sibling)]

    arrive(e_swap)
    here = field[:A, :].astype(BF).astype(F32)
    there = e_in[...].astype(F32)
    potential = by_core(here, there).astype(BF)[:, :64]
    grad_charge = by_core(there, here).astype(BF)[:, :64]
    out[0:A, :] = alive * (short_range + nn(potential, fw[...]))
    out[A : 2 * A, :] = alive * (short_grad + nn(grad_charge, cw[...]))

    arrive(h_swap)
    here, there = h2[...].astype(F32), h_in[...].astype(F32)
    out[6 * C : 6 * C + 64, :] = by_core(here, there) * grad_scale
    out[6 * C + 64 : 7 * C, :] = by_core(there, here) * grad_scale

    arrive(g_ys)
    g_xs = spread(gfull, x * gx, gx, nx, x_peer)
    arrive(g_xs)
    out[2 * C : 6 * C, :] = gfull[...].astype(F32) * grad_scale

    for copy in sent:
        copy.wait_send()


def place(
    rows, o_layer, o_feat, o_sg, o_tg, o_eg, o_mg, o_cg, o_fg, layer, feat, sem
):
    layer[...] = rows[0:A, :].astype(BF)
    feat[...] = rows[A : 2 * A, :].astype(BF)
    moves = [(layer, o_layer), (feat, o_feat)]
    moves += [
        (rows.at[pl.ds((i + 2) * C, C)], out) for i, out in enumerate((o_sg, o_tg, o_eg, o_mg))
    ]
    moves += [(rows.at[pl.ds(6 * C, 64)], o_cg), (rows.at[pl.ds(6 * C + 64, 64)], o_fg)]
    copies = [pltpu.make_async_copy(a, b, sem.at[i]) for i, (a, b) in enumerate(moves)]
    for copy in copies:
        copy.start()
    for copy in copies:
        copy.wait()


def local(
    features, positions, neighbours, distances, ghost_rows, atom_counts, wavevectors,
    wave_weights, source_weight, target_weight, edge_weight, mix_weight, charge_weight,
    field_weight, cotangent,
):
    geo = GEOMETRY
    nx, ny, nc, nz = geo["x"], geo["y"], geo["core"], geo["z_lo"] * geo["z_hi"]
    total_atoms = A * lax.axis_size("dx") * lax.axis_size("dy")
    factor_scale = 4.0 / math.sqrt(total_atoms * K)
    grad_scale = 1.0 / math.sqrt(total_atoms)
    a1, b1, c1 = ROWS[0] // nx, ROWS[1] // ny, ROWS[2] // nz
    a2, b2, c2 = a1 // ny, b1 // nx, c1 // nx
    last = a2 + b2 + c2
    gx, gy = 4 * C // nx, 4 * C // (nx * ny)

    def bf(*shape):
        return pltpu.VMEM(shape, BF)

    def f32(*shape):
        return pltpu.VMEM(shape, F32)

    scratch = [
        bf(A, C), bf(A, C), f32(8, A), f32(8, A), f32(8, K), bf(K, 2 * C),
        bf(nx - 1, a1, 2 * C), bf(a1, 2 * C),
        bf(ny - 1, b1, 2 * C), bf(b1, 2 * C),
        bf(nz - 1, c1, 2 * C), bf(c1, 2 * C),
        bf(ny - 1, a2, 2 * C), bf(nx - 1, b2, 2 * C), bf(nx - 1, c2, 2 * C),
        bf(last, 2 * C), bf(nz, a2 + b2, 2 * C), bf(ny, c2, 2 * C), bf(last, 2 * C),
        bf(last, C), bf(last, C), bf(K, C), bf(2 * A, K), bf(2 * A, K), bf(A, C), bf(A, C),
        bf(A, C), bf(A, C), bf(A, C), bf(A, C),
        bf(4 * C, C), bf(nx - 1, gx, C), bf(gx, C), bf(ny - 1, gy, C), bf(gy, C),
        bf(nz * nc, gy, C), bf(4 * C, C),
        bf(ny, 64, C), bf(nz, 64, C), bf(nx, 64, C), bf(64, C), bf(64, C),
        f32(NB, A), f32(NB, A), f32(C, A), f32(C, A), bf(C, 2 * A), f32(A, A),
        f32(C, A), f32(C, A), f32(2 * A, C), f32(C, C),
        pltpu.SemaphoreType.DMA((COPIES,)),
        pltpu.SemaphoreType.DMA((COPIES,)),
    ]
    vmem = pl.BlockSpec(memory_space=pltpu.VMEM)
    anywhere = pl.BlockSpec(memory_space=pl.ANY)
    operands = (
        features, positions, neighbours.T, distances.T, ghost_rows, atom_counts, wavevectors,
        wave_weights.reshape(1, K), source_weight, target_weight, edge_weight, mix_weight,
        charge_weight.T, field_weight, cotangent,
    )
    n_in = len(operands)
    held = [
        pltpu.SMEM(a.shape, a.dtype) if a.ndim == 1 else pltpu.VMEM(a.shape, a.dtype)
        for a in operands
    ]

    def kernel(*refs):
        left = refs[n_in + 1 :]
        body(factor_scale, grad_scale, refs[:n_in], refs[n_in], left[:n_in], *left[n_in:])

    rows = pl.pallas_call(
        kernel,
        out_shape=jax.ShapeDtypeStruct((7 * C, C), F32),
        in_specs=[anywhere] * n_in,
        out_specs=vmem,
        scratch_shapes=held + [pltpu.SemaphoreType.DMA((n_in,))] + scratch,
        compiler_params=pltpu.CompilerParams(
            collective_id=0, has_side_effects=True, vmem_limit_bytes=60 * 1024 * 1024
        ),
        name="ewald_layer",
    )(*operands)
    outs = pl.pallas_call(
        place,
        out_shape=[jax.ShapeDtypeStruct((A, C), BF)] * 2
        + [jax.ShapeDtypeStruct((C, C), F32)] * 4
        + [jax.ShapeDtypeStruct((64, C), F32)] * 2,
        in_specs=[vmem],
        out_specs=[anywhere] * 8,
        scratch_shapes=[bf(A, C), bf(A, C), pltpu.SemaphoreType.DMA((8,))],
        name="place_outputs",
    )(rows)
    return (*outs[:6], outs[6].T, outs[7])


def solution(mesh):
    atoms = P(("dx", "dy"), None)
    in_specs = (
        atoms, P(None, ("dx", "dy")), atoms, atoms, P(None, ("dx", "dy")), P(("dx", "dy")),
        P(), P(), P(), P(), P(), P(), P(), P(), atoms,
    )
    out_specs = (atoms, atoms, P(), P(), P(), P(), P(), P())
    return jax.shard_map(
        local, mesh=mesh, in_specs=in_specs, out_specs=out_specs, check_vma=False
    )
```

```python
import math

import jax
import jax.numpy as jnp
from jax import lax
from jax.experimental import pallas as pl
from jax.experimental.pallas import tpu as pltpu
from jax.sharding import PartitionSpec as P

GEOMETRY = dict(y=8, z_hi=4, x=4, z_lo=2, core=2)
K = 2048
C = 128
A = 128
NB = 64
STEP = 16
COPIES = 140
ROWS = (1024, 512, 512)

FIRST = (0, 14, 4, 5, 1, 6, 7)
LATER = (2, 3, 8, 9, 10, 11, 12, 13)

BF = jnp.bfloat16
F32 = jnp.float32


def nn(a, b):
    return lax.dot_general(a, b, (((1,), (0,)), ((), ())), preferred_element_type=F32)


def nt(a, b):
    return lax.dot_general(a, b, (((1,), (1,)), ((), ())), preferred_element_type=F32)


def half_turns(f):
    q = f * f
    s = 0.10982452
    for c in (-0.84611165, 3.60635422, -7.30824569, 4.44288292):
        s = s * q + c
    c0 = 0.31068803
    for c in (-1.88355791, 5.73946038, -6.97885095, 1.4142135):
        c0 = c0 * q + c
    return s * f, c0


def body(
    factor_scale,
    grad_scale,
    operands,
    out,
    held, held_sem,
    x_out, x_in, pos_out, pos_in, kv, sums,
    la, ta, lb, tb, lc, tc, la2, lb2, lc2, t2, lz, ly, fin,
    w_out, w_in, w_full, cosine, sine, e_out, e_in,
    gout, gin, ggout, gret,
    g0, rgx, g1, rgy, g2, rgz, gfull,
    rhy, rhz, rhx, h2, h_in,
    picks, hiddens, slopes, inners, pairs,
    nbr_t, gate_t, src_t, ga_t, tab_t, pick_t, agg_t, gs_t, tsum, epart,
    ssem, rsem,
):
    fetch = [
        pltpu.make_async_copy(src, dst, held_sem.at[i])
        for i, (src, dst) in enumerate(zip(operands, held))
    ]
    for i in FIRST + LATER:
        fetch[i].start()
    feat, pos, nbr, dist, ghost, counts, kvec, kw, sw, tw, ew, mw, cw, fw, cot = held

    geo = GEOMETRY
    nx, ny, nc = geo["x"], geo["y"], geo["core"]
    nzl, nzh = geo["z_lo"], geo["z_hi"]
    nz = nzl * nzh
    ndx, ndy = ny * nzh * nx, nzl * nc
    dx, dy = lax.axis_index("dx"), lax.axis_index("dy")
    x = lax.rem(dx, nx)
    zh = lax.rem(lax.div(dx, nx), nzh)
    y = lax.div(dx, nx * nzh)
    zl, core = lax.div(dy, nc), lax.rem(dy, nc)
    z = zh * nzl + zl

    def device(px=None, py=None, pz=None, pc=None):
        px = x if px is None else px
        py = y if py is None else py
        pz = z if pz is None else pz
        pc = core if pc is None else pc
        return (
            (py * nzh + lax.div(pz, nzl)) * nx + px,
            lax.rem(pz, nzl) * nc + pc,
        )

    def ahead(me, d, n):
        return lax.rem(me + d, n)

    def x_peer(d):
        return device(px=ahead(x, d, nx))

    def y_peer(d):
        return device(py=ahead(y, d, ny))

    def z_peer(d):
        return device(pz=ahead(z, d, nz))

    def zc_peer(d):
        return device(pz=ahead(z, d // nc, nz), pc=ahead(core, d % nc, nc))

    sibling = device(pc=ahead(core, 1, nc))
    faces = (
        (ahead(dx, 1, ndx), dy),
        (ahead(dx, ndx - 1, ndx), dy),
        (dx, ahead(dy, 1, ndy)),
        (dx, ahead(dy, ndy - 1, ndy)),
    )
    back = (faces[1], faces[0], faces[3], faces[2])

    barrier = pltpu.get_barrier_semaphore()
    greeted = list(faces)
    greeted += [x_peer(d) for d in range(1, nx)]
    greeted += [y_peer(d) for d in range(1, ny)]
    greeted += [zc_peer(d) for d in range(1, nz * nc)]
    for other in greeted:
        pl.semaphore_signal(
            barrier, inc=1, device_id=other, device_id_type=pl.DeviceIdType.MESH
        )

    sent = []

    def send(src, dst, other):
        slot = len(sent)
        copy = pltpu.make_async_remote_copy(
            src_ref=src,
            dst_ref=dst,
            send_sem=ssem.at[slot],
            recv_sem=rsem.at[slot],
            device_id=other,
            device_id_type=pl.DeviceIdType.MESH,
        )
        copy.start()
        sent.append(copy)
        return copy

    def arrive(copies):
        for copy in copies:
            copy.wait_recv()

    def rows(ref, start, size):
        return ref.at[pl.ds(pl.multiple_of(start, 16), size)]

    def scatter(src, base, landing, me, n, size, peer):
        return [
            send(rows(src, base + ahead(me, d, n) * size, size), landing.at[d - 1], peer(d))
            for d in range(1, n)
        ]

    def collect(src, base, landing, me, n, size, dst, dst_base=0):
        chunk = min(size, 128)

        def add(i, _):
            at = pl.multiple_of(i * chunk, 16)
            total = src[pl.ds(pl.multiple_of(base + me * size + at, 16), chunk), :].astype(F32)
            for d in range(1, n):
                total += landing[d - 1, pl.ds(at, chunk), :].astype(F32)
            dst[pl.ds(pl.multiple_of(dst_base + at, 16), chunk), :] = total.astype(BF)
            return 0

        if size == chunk:
            add(0, 0)
        else:
            lax.fori_loop(0, size // chunk, add, 0)

    def share(landing, me, n, peer):
        return [send(landing.at[me], landing.at[me], peer(d)) for d in range(1, n)]

    def summed_slots(landing, n):
        total = landing[0].astype(F32)
        for d in range(1, n):
            total += landing[d].astype(F32)
        return total

    def spread(ref, start, size, n, peer):
        return [
            send(rows(ref, start, size), rows(ref, start, size), peer(d)) for d in range(1, n)
        ]

    first_core = jnp.where(core == 0, 1.0, 0.0).astype(F32)

    def by_core(mine_if_first, mine_if_second):
        return first_core * mine_if_first + (1.0 - first_core) * mine_if_second

    for i in FIRST:
        fetch[i].wait()

    row_id = lax.broadcasted_iota(jnp.int32, (A, C), 0)
    alive = jnp.where(row_id < counts[0], 1.0, 0.0).astype(F32)
    masked32 = feat[...].astype(F32) * alive
    gm32 = cot[...].astype(F32) * alive
    masked, gm = masked32.astype(BF), gm32.astype(BF)
    for f in range(4):
        pick_t[:, f * 32 : (f + 1) * 32] = jnp.where(
            lax.broadcasted_iota(jnp.int32, (A, 32), 0) == ghost[f : f + 1, :], 1.0, 0.0
        )
    gout[...] = nn(pick_t[...].T.astype(BF), masked).astype(BF)
    x_out[...] = by_core(gm32, masked32).astype(BF)
    pos_out[...] = jnp.zeros_like(pos_out)
    pos_out[0:3, :] = pos[...]

    own_kind = by_core(masked32, gm32).astype(BF)
    kv[...] = jnp.zeros_like(kv)
    kv[0:3, :] = kvec[...] * (1.0 / (2.0 * math.pi))
    kv[3:4, :] = jnp.sqrt(kw[...] * factor_scale)

    def waves(turns, root):
        s, c = half_turns(turns - jnp.round(turns))
        s_root = s * root
        return (root - s * s_root).astype(BF), (c * s_root).astype(BF)

    def add_waves(first_row, place, start, stop):
        spots = [jnp.broadcast_to(place[a : a + 1, :], (A, A)).T for a in range(3)]
        spots = [jnp.concatenate([spot, spot], axis=1) for spot in spots]
        atoms = slice(first_row, first_row + A)

        def wave_block(block, _):
            at = pl.ds(pl.multiple_of(block * 256, 256), 256)
            turns = spots[0] * kv[0:1, at] + spots[1] * kv[1:2, at] + spots[2] * kv[2:3, at]
            cosine[atoms, at], sine[atoms, at] = waves(turns, kv[3:4, at])
            return 0

        lax.fori_loop(start // 256, stop // 256, wave_block, 0)

    add_waves(0, pos_out, 0, K)
    own_t = own_kind.astype(F32).T

    pl.semaphore_wait(barrier, len(greeted))
    atoms_in = [send(x_out, x_in, sibling), send(pos_out, pos_in, sibling)]
    ghosts_in = [
        send(gout.at[pl.ds(f * 32, 32)], gin.at[pl.ds(f * 32, 32)], faces[f]) for f in range(4)
    ]
    for i in LATER:
        fetch[i].wait()

    masked_t = masked32.T.astype(BF)

    arrive(atoms_in)

    values_t = jnp.concatenate([own_t, x_in[...].astype(F32).T], axis=1).astype(BF)

    def sum_block(block, _):
        at = pl.ds(pl.multiple_of(block * 512, 512), 512)
        of_cos = nn(values_t, cosine[:, at]).astype(BF)
        of_sin = nn(values_t, sine[:, at]).astype(BF)
        sums[at, :C] = of_cos.T
        sums[at, C:] = of_sin.T
        return 0

    def add_sums(start, stop):
        add_waves(A, pos_in, start, stop)
        lax.fori_loop(start // 512, stop // 512, sum_block, 0)

    base_a, base_b, base_c = 0, ROWS[0], ROWS[0] + ROWS[1]
    a1, b1, c1 = ROWS[0] // nx, ROWS[1] // ny, ROWS[2] // nz
    a2, b2, c2 = a1 // ny, b1 // nx, c1 // nx
    add_sums(0, base_b)
    first_a = scatter(sums, base_a, la, x, nx, a1, x_peer)
    add_sums(base_b, base_c)
    first_b = scatter(sums, base_b, lb, y, ny, b1, y_peer)
    add_sums(base_c, K)
    first_c = scatter(sums, base_c, lc, z, nz, c1, z_peer)

    src_t[...] = nn(masked, sw[...]).astype(BF).astype(F32).T
    ga_t[...] = nt(gm, mw[...]).astype(BF).astype(F32).T
    nbr_t[...] = nbr[...].astype(F32)
    s, c = half_turns(dist[...] * 0.1)
    gate_t[...] = jnp.where(nbr[...] < 2 * A, 0.5 * c * c, 0.0)
    tab_t[:, :A] = nn(masked, tw[...]).astype(BF).astype(F32).T.astype(BF)
    agg_t[...] = jnp.zeros_like(agg_t)
    gs_t[...] = jnp.zeros_like(gs_t)
    tsum[...] = jnp.zeros_like(tsum)
    epart[...] = jnp.zeros_like(epart)
    ew_t = ew[...].astype(F32).T.astype(BF)
    table_row = lax.broadcasted_iota(jnp.int32, (2 * A, A), 0).astype(F32).astype(BF)

    arrive(ghosts_in)
    ghosts = gin[...]
    tab_t[:, A:] = nn(ghosts, tw[...]).astype(BF).astype(F32).T.astype(BF)
    table_t = jnp.concatenate([masked_t, ghosts.astype(F32).T.astype(BF)], axis=1)

    def edge_step(step, _):
        slots = [(pl.ds(step * STEP + j, 1), slice(j * A, (j + 1) * A)) for j in range(STEP)]
        for row, at in slots:
            named = jnp.broadcast_to(nbr_t[row, :], (2 * A, A)).astype(BF)
            picks[:, at] = jnp.where(table_row == named, jnp.ones((), BF), jnp.zeros((), BF))
        summed = nn(tab_t[...], picks[...])
        for row, at in slots:
            v = summed[:, at] + src_t[...]
            g = 0.5 * jnp.tanh(0.5 * v) + 0.5
            hidden = v * g
            hiddens[:, at] = hidden.astype(BF)
            slopes[:, at] = g + hidden * (1.0 - g)
        mixed = nn(ew_t, hiddens[...])
        agg_sum = agg_t[...]
        for row, at in slots:
            v = mixed[:, at]
            g = 0.5 * jnp.tanh(0.5 * v) + 0.5
            message = v * g
            agg_sum += gate_t[row, :] * message
            inners[:, at] = (gate_t[row, :] * ga_t[...] * (g + message * (1.0 - g))).astype(BF)
        agg_t[...] = agg_sum
        outer = nn(ew[...], inners[...])
        gs_sum = gs_t[...]
        for row, at in slots:
            pair_grad = outer[:, at] * slopes[:, at]
            gs_sum += pair_grad
            pairs[:, at] = pair_grad.astype(BF)
        gs_t[...] = gs_sum
        epart[...] += nt(hiddens[...], inners[...])
        tsum[...] += nt(picks[...], pairs[...])
        return 0

    steps = NB // STEP
    lax.fori_loop(0, steps - 1, edge_step, 0)
    arrive(first_a)
    collect(sums, base_a, la, x, nx, a1, ta)
    second_a = scatter(ta, 0, la2, y, ny, a2, y_peer)
    arrive(first_b)
    collect(sums, base_b, lb, y, ny, b1, tb)
    second_b = scatter(tb, 0, lb2, x, nx, b2, x_peer)
    arrive(first_c)
    collect(sums, base_c, lc, z, nz, c1, tc)
    second_c = scatter(tc, 0, lc2, x, nx, c2, x_peer)

    lax.fori_loop(steps - 1, steps, edge_step, 0)
    table_sum = tsum[...]
    ggout[...] = table_sum[A:, :].astype(BF)
    ghosts_back = [
        send(ggout.at[pl.ds(f * 32, 32)], gret.at[pl.ds(f * 32, 32)], back[f]) for f in range(4)
    ]
    aggregate_t = agg_t[...].astype(BF)
    grad_source = gs_t[...].T.astype(BF)
    g0[0:C, :] = nn(masked_t, grad_source).astype(BF)
    g0[C : 2 * C, :] = nn(table_t, table_sum.astype(BF)).astype(BF)
    g0[2 * C : 3 * C, :] = epart[...].astype(BF)
    g0[3 * C :, :] = nn(aggregate_t, gm).astype(BF)
    gx, gy = 4 * C // nx, 4 * C // (nx * ny)
    g_x = scatter(g0, 0, rgx, x, nx, gx, x_peer)

    ab2 = a2 + b2
    arrive(second_b)
    collect(tb, 0, lb2, x, nx, b2, t2, a2)
    arrive(second_c)
    collect(tc, 0, lc2, x, nx, c2, t2, ab2)
    ly[pl.ds(y, 1)] = t2[ab2:, :][None]
    third_c = share(ly, y, ny, y_peer)
    arrive(second_a)
    collect(ta, 0, la2, y, ny, a2, t2, 0)
    lz[pl.ds(z, 1)] = t2[:ab2, :][None]
    third_ab = share(lz, z, nz, z_peer)

    arrive(g_x)
    collect(g0, 0, rgx, x, nx, gx, g1)
    g_y = scatter(g1, 0, rgy, y, ny, gy, y_peer)

    arrive(ghosts_back)
    grad_target = (table_sum[:A, :] + nn(pick_t[...].astype(BF), gret[...])).astype(BF)
    short_grad = nt(grad_source, sw[...]) + nt(grad_target, tw[...])
    short_range = nn(agg_t[...].T.astype(BF), mw[...])

    fw_t = fw[...].astype(F32).T
    project = by_core(cw[...].astype(F32).T, fw_t).astype(BF)
    none = jnp.zeros((C, 64), BF)
    project = jnp.concatenate(
        [
            jnp.concatenate([project, none], axis=1),
            jnp.concatenate([none, project], axis=1),
        ],
        axis=0,
    )
    arrive(third_c)
    fin[ab2:, :] = summed_slots(ly, ny).astype(BF)
    arrive(third_ab)
    fin[:ab2, :] = summed_slots(lz, nz).astype(BF)
    w_out[...] = nn(fin[...], project).astype(BF)
    place_a = pl.multiple_of(base_a + x * a1 + y * a2, 16)
    place_b = pl.multiple_of(base_b + y * b1 + x * b2, 16)
    place_c = pl.multiple_of(base_c + z * c1 + x * c2, 16)
    w_full[pl.ds(place_a, a2), :] = w_out[:a2, :]
    w_full[pl.ds(place_b, b2), :] = w_out[a2:ab2, :]
    w_full[pl.ds(place_c, c2), :] = w_out[ab2:, :]
    spread_a = spread(w_full, place_a, a2, ny, y_peer)
    spread_b = spread(w_full, place_b, b2, nx, x_peer)
    spread_c = spread(w_full, place_c, c2, nx, x_peer)
    w_swap = [send(w_out, w_in, sibling)]

    arrive(w_swap)
    other_t = w_in[...].astype(F32).T
    in_ab = lax.broadcasted_iota(jnp.int32, other_t.shape, 1) < ab2

    def weight_part(left):
        quads = nn(left.astype(BF), fin[...])
        return (quads[:64, :C] + quads[64:, C:]).astype(BF)

    rhy[pl.ds(y, 1)] = weight_part(jnp.where(in_ab, other_t, 0.0))[None]
    rhz[pl.ds(z, 1)] = weight_part(jnp.where(in_ab, 0.0, other_t))[None]

    h_y = share(rhy, y, ny, y_peer)
    h_z = share(rhz, z, nz, z_peer)

    arrive(g_y)
    collect(g1, 0, rgy, y, ny, gy, g2)
    zc = z * nc + core
    rgz[pl.ds(zc, 1)] = g2[...][None]
    g_zc = share(rgz, zc, nz * nc, zc_peer)

    arrive(spread_b)
    spread_b = spread(w_full, base_b + y * b1, b1, ny, y_peer)
    arrive(spread_c)
    spread_c = spread(w_full, base_c + z * c1, c1, nz, z_peer)
    arrive(spread_a)
    spread_a = spread(w_full, base_a + x * a1, a1, nx, x_peer)

    arrive(h_y)
    arrive(h_z)
    rhx[pl.ds(x, 1)] = (summed_slots(rhy, ny) + summed_slots(rhz, nz)).astype(BF)[None]
    h_x = share(rhx, x, nx, x_peer)

    arrive(g_zc)
    g_mine = pl.multiple_of(x * gx + y * gy, 16)
    gfull[pl.ds(g_mine, gy), :] = summed_slots(rgz, nz * nc).astype(BF)
    g_ys = spread(gfull, g_mine, gy, ny, y_peer)

    def field_of(start, stop):
        at, weights = slice(start, stop), w_full[start:stop, :]
        return nn(cosine[:, at], weights), nn(sine[:, at], weights)

    arrive(spread_b)
    arrive(spread_c)
    of_cos, of_sin = field_of(base_b, K)
    arrive(spread_a)
    more_cos, more_sin = field_of(base_a, base_b)
    field = of_cos + more_cos + pltpu.roll(of_sin + more_sin, 64, 1)
    e_out[...] = field[A:, :].astype(BF)
    e_swap = [send(e_out, e_in, sibling)]

    arrive(g_ys)
    g_xs = spread(gfull, x * gx, gx, nx, x_peer)

    arrive(h_x)
    h2[...] = summed_slots(rhx, nx).astype(BF)
    h_swap = [send(h2, h_in, sibling)]

    arrive(e_swap)
    here = field[:A, :].astype(BF).astype(F32)
    there = e_in[...].astype(F32)
    potential = by_core(here, there).astype(BF)[:, :64]
    grad_charge = by_core(there, here).astype(BF)[:, :64]
    out[0:A, :] = alive * (short_range + nn(potential, fw[...]))
    out[A : 2 * A, :] = alive * (short_grad + nn(grad_charge, cw[...]))

    arrive(h_swap)
    here, there = h2[...].astype(F32), h_in[...].astype(F32)
    out[6 * C : 6 * C + 64, :] = by_core(here, there) * grad_scale
    out[6 * C + 64 : 7 * C, :] = by_core(there, here) * grad_scale

    arrive(g_xs)
    out[2 * C : 6 * C, :] = gfull[...].astype(F32) * grad_scale

    for copy in sent:
        copy.wait_send()


def place(
    rows, o_layer, o_feat, o_sg, o_tg, o_eg, o_mg, o_cg, o_fg, layer, feat, sem
):
    layer[...] = rows[0:A, :].astype(BF)
    feat[...] = rows[A : 2 * A, :].astype(BF)
    moves = [(layer, o_layer), (feat, o_feat)]
    moves += [
        (rows.at[pl.ds((i + 2) * C, C)], out) for i, out in enumerate((o_sg, o_tg, o_eg, o_mg))
    ]
    moves += [(rows.at[pl.ds(6 * C, 64)], o_cg), (rows.at[pl.ds(6 * C + 64, 64)], o_fg)]
    copies = [pltpu.make_async_copy(a, b, sem.at[i]) for i, (a, b) in enumerate(moves)]
    for copy in copies:
        copy.start()
    for copy in copies:
        copy.wait()


def local(
    features, positions, neighbours, distances, ghost_rows, atom_counts, wavevectors,
    wave_weights, source_weight, target_weight, edge_weight, mix_weight, charge_weight,
    field_weight, cotangent,
):
    geo = GEOMETRY
    nx, ny, nc, nz = geo["x"], geo["y"], geo["core"], geo["z_lo"] * geo["z_hi"]
    total_atoms = A * lax.axis_size("dx") * lax.axis_size("dy")
    factor_scale = 4.0 / math.sqrt(total_atoms * K)
    grad_scale = 1.0 / math.sqrt(total_atoms)
    a1, b1, c1 = ROWS[0] // nx, ROWS[1] // ny, ROWS[2] // nz
    a2, b2, c2 = a1 // ny, b1 // nx, c1 // nx
    last = a2 + b2 + c2
    gx, gy = 4 * C // nx, 4 * C // (nx * ny)

    def bf(*shape):
        return pltpu.VMEM(shape, BF)

    def f32(*shape):
        return pltpu.VMEM(shape, F32)

    scratch = [
        bf(A, C), bf(A, C), f32(8, A), f32(8, A), f32(8, K), bf(K, 2 * C),
        bf(nx - 1, a1, 2 * C), bf(a1, 2 * C),
        bf(ny - 1, b1, 2 * C), bf(b1, 2 * C),
        bf(nz - 1, c1, 2 * C), bf(c1, 2 * C),
        bf(ny - 1, a2, 2 * C), bf(nx - 1, b2, 2 * C), bf(nx - 1, c2, 2 * C),
        bf(last, 2 * C), bf(nz, a2 + b2, 2 * C), bf(ny, c2, 2 * C), bf(last, 2 * C),
        bf(last, C), bf(last, C), bf(K, C), bf(2 * A, K), bf(2 * A, K), bf(A, C), bf(A, C),
        bf(A, C), bf(A, C), bf(A, C), bf(A, C),
        bf(4 * C, C), bf(nx - 1, gx, C), bf(gx, C), bf(ny - 1, gy, C), bf(gy, C),
        bf(nz * nc, gy, C), bf(4 * C, C),
        bf(ny, 64, C), bf(nz, 64, C), bf(nx, 64, C), bf(64, C), bf(64, C),
        bf(2 * A, STEP * A), bf(C, STEP * A), f32(C, STEP * A),
        bf(C, STEP * A), bf(C, STEP * A),
        f32(NB, A), f32(NB, A), f32(C, A), f32(C, A), bf(C, 2 * A), f32(A, A),
        f32(C, A), f32(C, A), f32(2 * A, C), f32(C, C),
        pltpu.SemaphoreType.DMA((COPIES,)),
        pltpu.SemaphoreType.DMA((COPIES,)),
    ]
    vmem = pl.BlockSpec(memory_space=pltpu.VMEM)
    anywhere = pl.BlockSpec(memory_space=pl.ANY)
    operands = (
        features, positions, neighbours.T, distances.T, ghost_rows, atom_counts, wavevectors,
        wave_weights.reshape(1, K), source_weight, target_weight, edge_weight, mix_weight,
        charge_weight.T, field_weight, cotangent,
    )
    n_in = len(operands)
    held = [
        pltpu.SMEM(a.shape, a.dtype) if a.ndim == 1 else pltpu.VMEM(a.shape, a.dtype)
        for a in operands
    ]

    def kernel(*refs):
        left = refs[n_in + 1 :]
        body(factor_scale, grad_scale, refs[:n_in], refs[n_in], left[:n_in], *left[n_in:])

    rows = pl.pallas_call(
        kernel,
        out_shape=jax.ShapeDtypeStruct((7 * C, C), F32),
        in_specs=[anywhere] * n_in,
        out_specs=vmem,
        scratch_shapes=held + [pltpu.SemaphoreType.DMA((n_in,))] + scratch,
        compiler_params=pltpu.CompilerParams(
            collective_id=0, has_side_effects=True, vmem_limit_bytes=60 * 1024 * 1024
        ),
        name="ewald_layer",
    )(*operands)
    outs = pl.pallas_call(
        place,
        out_shape=[jax.ShapeDtypeStruct((A, C), BF)] * 2
        + [jax.ShapeDtypeStruct((C, C), F32)] * 4
        + [jax.ShapeDtypeStruct((64, C), F32)] * 2,
        in_specs=[vmem],
        out_specs=[anywhere] * 8,
        scratch_shapes=[bf(A, C), bf(A, C), pltpu.SemaphoreType.DMA((8,))],
        name="place_outputs",
    )(rows)
    return (*outs[:6], outs[6].T, outs[7])


def solution(mesh):
    atoms = P(("dx", "dy"), None)
    in_specs = (
        atoms, P(None, ("dx", "dy")), atoms, atoms, P(None, ("dx", "dy")), P(("dx", "dy")),
        P(), P(), P(), P(), P(), P(), P(), P(), atoms,
    )
    out_specs = (atoms, atoms, P(), P(), P(), P(), P(), P())
    return jax.shard_map(
        local, mesh=mesh, in_specs=in_specs, out_specs=out_specs, check_vma=False
    )
```

```python
import math

import jax
import jax.numpy as jnp
from jax import lax
from jax.experimental import pallas as pl
from jax.experimental.pallas import tpu as pltpu
from jax.sharding import PartitionSpec as P

GEOMETRY = dict(y=8, z_hi=4, x=4, z_lo=2, core=2)
K = 2048
C = 128
A = 128
NB = 64
STEP = 16
COPIES = 140
ROWS = (1024, 512, 512)

FIRST = (0, 14, 4, 5, 1, 6, 7)
LATER = (2, 3, 8, 9, 10, 11, 12, 13)

BF = jnp.bfloat16
F32 = jnp.float32


def nn(a, b):
    return lax.dot_general(a, b, (((1,), (0,)), ((), ())), preferred_element_type=F32)


def nt(a, b):
    return lax.dot_general(a, b, (((1,), (1,)), ((), ())), preferred_element_type=F32)


def half_turns(f):
    q = f * f
    s = 0.10982452
    for c in (-0.84611165, 3.60635422, -7.30824569, 4.44288292):
        s = s * q + c
    c0 = 0.31068803
    for c in (-1.88355791, 5.73946038, -6.97885095, 1.4142135):
        c0 = c0 * q + c
    return s * f, c0


def body(
    factor_scale,
    grad_scale,
    operands,
    out,
    held, held_sem,
    x_out, x_in, pos_out, pos_in, kv, sums,
    la, ta, lb, tb, lc, tc, la2, lb2, lc2, t2, lz, ly, fin,
    w_out, w_in, w_full, cosine, sine, e_out, e_in,
    gout, gin, ggout, gret,
    g0, rgx, g1, rgy, rgz, gfull,
    rhy, rhz, rhx, h2, h_in,
    picks, hiddens, slopes, inners, pairs,
    nbr_t, gate_t, src_t, ga_t, tab_t, pick_t, agg_t, gs_t, tsum, epart,
    ssem, rsem,
):
    fetch = [
        pltpu.make_async_copy(src, dst, held_sem.at[i])
        for i, (src, dst) in enumerate(zip(operands, held))
    ]
    for i in FIRST + LATER:
        fetch[i].start()
    feat, pos, nbr, dist, ghost, counts, kvec, kw, sw, tw, ew, mw, cw, fw, cot = held

    geo = GEOMETRY
    nx, ny, nc = geo["x"], geo["y"], geo["core"]
    nzl, nzh = geo["z_lo"], geo["z_hi"]
    nz = nzl * nzh
    ndx, ndy = ny * nzh * nx, nzl * nc
    dx, dy = lax.axis_index("dx"), lax.axis_index("dy")
    x = lax.rem(dx, nx)
    zh = lax.rem(lax.div(dx, nx), nzh)
    y = lax.div(dx, nx * nzh)
    zl, core = lax.div(dy, nc), lax.rem(dy, nc)
    z = zh * nzl + zl

    def device(px=None, py=None, pz=None, pc=None):
        px = x if px is None else px
        py = y if py is None else py
        pz = z if pz is None else pz
        pc = core if pc is None else pc
        return (
            (py * nzh + lax.div(pz, nzl)) * nx + px,
            lax.rem(pz, nzl) * nc + pc,
        )

    def ahead(me, d, n):
        return lax.rem(me + d, n)

    def x_peer(d):
        return device(px=ahead(x, d, nx))

    def y_peer(d):
        return device(py=ahead(y, d, ny))

    def z_peer(d):
        return device(pz=ahead(z, d, nz))

    def xc_peer(d):
        return device(px=ahead(x, d // nc, nx), pc=ahead(core, d % nc, nc))

    sibling = device(pc=ahead(core, 1, nc))
    faces = (
        (ahead(dx, 1, ndx), dy),
        (ahead(dx, ndx - 1, ndx), dy),
        (dx, ahead(dy, 1, ndy)),
        (dx, ahead(dy, ndy - 1, ndy)),
    )
    back = (faces[1], faces[0], faces[3], faces[2])

    barrier = pltpu.get_barrier_semaphore()
    greeted = list(faces)
    greeted += [xc_peer(d) for d in range(1, nx * nc)]
    greeted += [y_peer(d) for d in range(1, ny)]
    greeted += [z_peer(d) for d in range(1, nz)]
    for other in greeted:
        pl.semaphore_signal(
            barrier, inc=1, device_id=other, device_id_type=pl.DeviceIdType.MESH
        )

    sent = []

    def send(src, dst, other):
        slot = len(sent)
        copy = pltpu.make_async_remote_copy(
            src_ref=src,
            dst_ref=dst,
            send_sem=ssem.at[slot],
            recv_sem=rsem.at[slot],
            device_id=other,
            device_id_type=pl.DeviceIdType.MESH,
        )
        copy.start()
        sent.append(copy)
        return copy

    def arrive(copies):
        for copy in copies:
            copy.wait_recv()

    settled = []

    def settle(upto):
        for copy in sent[len(settled) : upto]:
            copy.wait_send()
            settled.append(copy)

    def rows(ref, start, size):
        return ref.at[pl.ds(pl.multiple_of(start, 16), size)]

    def scatter(src, base, landing, me, n, size, peer):
        return [
            send(rows(src, base + ahead(me, d, n) * size, size), landing.at[d - 1], peer(d))
            for d in range(1, n)
        ]

    def collect(src, base, landing, me, n, size, dst, dst_base=0):
        chunk = min(size, 128)

        def add(i, _):
            at = pl.multiple_of(i * chunk, 16)
            total = src[pl.ds(pl.multiple_of(base + me * size + at, 16), chunk), :].astype(F32)
            for d in range(1, n):
                total += landing[d - 1, pl.ds(at, chunk), :].astype(F32)
            dst[pl.ds(pl.multiple_of(dst_base + at, 16), chunk), :] = total.astype(BF)
            return 0

        if size == chunk:
            add(0, 0)
        else:
            lax.fori_loop(0, size // chunk, add, 0)

    def share(landing, me, n, peer):
        return [send(landing.at[me], landing.at[me], peer(d)) for d in range(1, n)]

    def summed_slots(landing, n):
        total = landing[0].astype(F32)
        for d in range(1, n):
            total += landing[d].astype(F32)
        return total

    def spread(ref, start, size, n, peer):
        return [
            send(rows(ref, start, size), rows(ref, start, size), peer(d)) for d in range(1, n)
        ]

    first_core = jnp.where(core == 0, 1.0, 0.0).astype(F32)

    def by_core(mine_if_first, mine_if_second):
        return first_core * mine_if_first + (1.0 - first_core) * mine_if_second

    for i in FIRST:
        fetch[i].wait()

    row_id = lax.broadcasted_iota(jnp.int32, (A, C), 0)
    alive = jnp.where(row_id < counts[0], 1.0, 0.0).astype(F32)
    masked32 = feat[...].astype(F32) * alive
    gm32 = cot[...].astype(F32) * alive
    masked, gm = masked32.astype(BF), gm32.astype(BF)
    for f in range(4):
        pick_t[:, f * 32 : (f + 1) * 32] = jnp.where(
            lax.broadcasted_iota(jnp.int32, (A, 32), 0) == ghost[f : f + 1, :], 1.0, 0.0
        )
    gout[...] = nn(pick_t[...].T.astype(BF), masked).astype(BF)
    x_out[...] = by_core(gm32, masked32).astype(BF)
    pos_out[...] = jnp.zeros_like(pos_out)
    pos_out[0:3, :] = pos[...]

    own_kind = by_core(masked32, gm32).astype(BF)
    kv[...] = jnp.zeros_like(kv)
    kv[0:3, :] = kvec[...] * (1.0 / (2.0 * math.pi))
    kv[3:4, :] = jnp.sqrt(kw[...] * factor_scale)

    def waves(turns, root):
        s, c = half_turns(turns - jnp.round(turns))
        s_root = s * root
        return (root - s * s_root).astype(BF), (c * s_root).astype(BF)

    def add_waves(first_row, place, start, stop):
        spots = [jnp.broadcast_to(place[a : a + 1, :], (A, A)).T for a in range(3)]
        spots = [jnp.concatenate([spot, spot], axis=1) for spot in spots]
        atoms = slice(first_row, first_row + A)

        def wave_block(block, _):
            at = pl.ds(pl.multiple_of(block * 256, 256), 256)
            turns = spots[0] * kv[0:1, at] + spots[1] * kv[1:2, at] + spots[2] * kv[2:3, at]
            cosine[atoms, at], sine[atoms, at] = waves(turns, kv[3:4, at])
            return 0

        lax.fori_loop(start // 256, stop // 256, wave_block, 0)

    add_waves(0, pos_out, 0, K)
    own_t = own_kind.astype(F32).T

    for i in LATER:
        fetch[i].wait()

    masked_t = masked32.T.astype(BF)

    src_t[...] = nn(masked, sw[...]).astype(BF).astype(F32).T
    ga_t[...] = nt(gm, mw[...]).astype(BF).astype(F32).T
    nbr_t[...] = nbr[...].astype(F32)
    s, c = half_turns(dist[...] * 0.1)
    gate_t[...] = jnp.where(nbr[...] < 2 * A, 0.5 * c * c, 0.0)
    tab_t[:, :A] = nn(masked, tw[...]).astype(BF).astype(F32).T.astype(BF)
    agg_t[...] = jnp.zeros_like(agg_t)
    gs_t[...] = jnp.zeros_like(gs_t)
    tsum[...] = jnp.zeros_like(tsum)
    epart[...] = jnp.zeros_like(epart)
    ew_t = ew[...].astype(F32).T.astype(BF)

    pl.semaphore_wait(barrier, len(greeted))
    atoms_in = [send(x_out, x_in, sibling), send(pos_out, pos_in, sibling)]
    ghosts_in = [
        send(gout.at[pl.ds(f * 32, 32)], gin.at[pl.ds(f * 32, 32)], faces[f]) for f in range(4)
    ]
    arrive(atoms_in)

    values_t = jnp.concatenate([own_t, x_in[...].astype(F32).T], axis=1).astype(BF)

    def sum_block(block, _):
        at = pl.ds(pl.multiple_of(block * 512, 512), 512)
        of_cos = nn(values_t, cosine[:, at]).astype(BF)
        of_sin = nn(values_t, sine[:, at]).astype(BF)
        sums[at, :C] = of_cos.T
        sums[at, C:] = of_sin.T
        return 0

    def add_sums(start, stop):
        add_waves(A, pos_in, start, stop)
        lax.fori_loop(start // 512, stop // 512, sum_block, 0)

    base_a, base_b, base_c = 0, ROWS[0], ROWS[0] + ROWS[1]
    a1, b1, c1 = ROWS[0] // nx, ROWS[1] // ny, ROWS[2] // nz
    a2, b2, c2 = a1 // ny, b1 // nx, c1 // nx
    add_sums(0, base_b)
    first_a = scatter(sums, base_a, la, x, nx, a1, x_peer)
    add_sums(base_b, base_c)
    first_b = scatter(sums, base_b, lb, y, ny, b1, y_peer)
    add_sums(base_c, K)
    first_c = scatter(sums, base_c, lc, z, nz, c1, z_peer)

    table_row = lax.broadcasted_iota(jnp.int32, (2 * A, A), 0).astype(F32).astype(BF)

    arrive(ghosts_in)
    ghosts = gin[...]
    tab_t[:, A:] = nn(ghosts, tw[...]).astype(BF).astype(F32).T.astype(BF)
    table_t = jnp.concatenate([masked_t, ghosts.astype(F32).T.astype(BF)], axis=1)

    def edge_step(step, _):
        slots = [(pl.ds(step * STEP + j, 1), slice(j * A, (j + 1) * A)) for j in range(STEP)]
        for row, at in slots:
            named = jnp.broadcast_to(nbr_t[row, :], (2 * A, A)).astype(BF)
            picks[:, at] = jnp.where(table_row == named, jnp.ones((), BF), jnp.zeros((), BF))
        summed = nn(tab_t[...], picks[...])
        for row, at in slots:
            v = summed[:, at] + src_t[...]
            g = 0.5 * jnp.tanh(0.5 * v) + 0.5
            hidden = v * g
            hiddens[:, at] = hidden.astype(BF)
            slopes[:, at] = g + hidden * (1.0 - g)
        mixed = nn(ew_t, hiddens[...])
        agg_sum = agg_t[...]
        for row, at in slots:
            v = mixed[:, at]
            g = 0.5 * jnp.tanh(0.5 * v) + 0.5
            message = v * g
            agg_sum += gate_t[row, :] * message
            inners[:, at] = (gate_t[row, :] * ga_t[...] * (g + message * (1.0 - g))).astype(BF)
        agg_t[...] = agg_sum
        outer = nn(ew[...], inners[...])
        gs_sum = gs_t[...]
        for row, at in slots:
            pair_grad = outer[:, at] * slopes[:, at]
            gs_sum += pair_grad
            pairs[:, at] = pair_grad.astype(BF)
        gs_t[...] = gs_sum
        epart[...] += nt(hiddens[...], inners[...])
        tsum[...] += nt(picks[...], pairs[...])
        return 0

    steps = NB // STEP
    lax.fori_loop(0, steps - 1, edge_step, 0)
    first_count = len(sent)
    arrive(first_a)
    collect(sums, base_a, la, x, nx, a1, ta)
    second_a = scatter(ta, 0, la2, y, ny, a2, y_peer)
    arrive(first_b)
    collect(sums, base_b, lb, y, ny, b1, tb)
    second_b = scatter(tb, 0, lb2, x, nx, b2, x_peer)
    arrive(first_c)
    collect(sums, base_c, lc, z, nz, c1, tc)
    second_c = scatter(tc, 0, lc2, x, nx, c2, x_peer)

    lax.fori_loop(steps - 1, steps, edge_step, 0)
    table_sum = tsum[...]
    ggout[...] = table_sum[A:, :].astype(BF)
    ghosts_back = [
        send(ggout.at[pl.ds(f * 32, 32)], gret.at[pl.ds(f * 32, 32)], back[f]) for f in range(4)
    ]
    aggregate_t = agg_t[...].astype(BF)
    grad_source = gs_t[...].T.astype(BF)
    g0[0:C, :] = nn(masked_t, grad_source).astype(BF)
    g0[C : 2 * C, :] = nn(table_t, table_sum.astype(BF)).astype(BF)
    g0[2 * C : 3 * C, :] = epart[...].astype(BF)
    g0[3 * C :, :] = nn(aggregate_t, gm).astype(BF)
    gx = 4 * C // (nx * nc)
    xc = x * nc + core
    g_x = [
        send(
            rows(g0, (ahead(x, d // nc, nx) * nc + ahead(core, d % nc, nc)) * gx, gx),
            rgx.at[d - 1],
            xc_peer(d),
        )
        for d in range(1, nx * nc)
    ]

    second_count = len(sent)
    ab2 = a2 + b2
    settle(first_count)
    arrive(second_b)
    collect(tb, 0, lb2, x, nx, b2, t2, a2)
    arrive(second_c)
    collect(tc, 0, lc2, x, nx, c2, t2, ab2)
    ly[pl.ds(y, 1)] = t2[ab2:, :][None]
    third_c = share(ly, y, ny, y_peer)
    arrive(second_a)
    collect(ta, 0, la2, y, ny, a2, t2, 0)
    lz[pl.ds(z, 1)] = t2[:ab2, :][None]
    third_ab = share(lz, z, nz, z_peer)

    arrive(g_x)
    collect(g0, 0, rgx, xc, nx * nc, gx, g1)
    rgy[pl.ds(y, 1)] = g1[...][None]
    g_y = share(rgy, y, ny, y_peer)

    arrive(ghosts_back)
    grad_target = (table_sum[:A, :] + nn(pick_t[...].astype(BF), gret[...])).astype(BF)
    short_grad = nt(grad_source, sw[...]) + nt(grad_target, tw[...])
    short_range = nn(agg_t[...].T.astype(BF), mw[...])

    fw_t = fw[...].astype(F32).T
    project = by_core(cw[...].astype(F32).T, fw_t).astype(BF)
    none = jnp.zeros((C, 64), BF)
    project = jnp.concatenate(
        [
            jnp.concatenate([project, none], axis=1),
            jnp.concatenate([none, project], axis=1),
        ],
        axis=0,
    )
    third_count = len(sent)
    settle(second_count)
    arrive(third_c)
    fin[ab2:, :] = summed_slots(ly, ny).astype(BF)
    arrive(third_ab)
    fin[:ab2, :] = summed_slots(lz, nz).astype(BF)
    w_out[...] = nn(fin[...], project).astype(BF)
    place_a = pl.multiple_of(base_a + x * a1 + y * a2, 16)
    place_b = pl.multiple_of(base_b + y * b1 + x * b2, 16)
    place_c = pl.multiple_of(base_c + z * c1 + x * c2, 16)
    w_full[pl.ds(place_a, a2), :] = w_out[:a2, :]
    w_full[pl.ds(place_b, b2), :] = w_out[a2:ab2, :]
    w_full[pl.ds(place_c, c2), :] = w_out[ab2:, :]
    spread_a = spread(w_full, place_a, a2, ny, y_peer)
    spread_b = spread(w_full, place_b, b2, nx, x_peer)
    spread_c = spread(w_full, place_c, c2, nx, x_peer)
    w_swap = [send(w_out, w_in, sibling)]

    arrive(w_swap)
    other_t = w_in[...].astype(F32).T
    in_ab = lax.broadcasted_iota(jnp.int32, other_t.shape, 1) < ab2

    def weight_part(left):
        quads = nn(left.astype(BF), fin[...])
        return (quads[:64, :C] + quads[64:, C:]).astype(BF)

    rhy[pl.ds(y, 1)] = weight_part(jnp.where(in_ab, other_t, 0.0))[None]
    rhz[pl.ds(z, 1)] = weight_part(jnp.where(in_ab, 0.0, other_t))[None]

    h_y = share(rhy, y, ny, y_peer)
    h_z = share(rhz, z, nz, z_peer)

    arrive(g_y)
    rgz[pl.ds(z, 1)] = summed_slots(rgy, ny).astype(BF)[None]
    g_z = share(rgz, z, nz, z_peer)

    settle(third_count)
    fourth_count = len(sent)
    arrive(spread_b)
    spread_b = spread(w_full, base_b + y * b1, b1, ny, y_peer)
    arrive(spread_c)
    spread_c = spread(w_full, base_c + z * c1, c1, nz, z_peer)
    arrive(spread_a)
    spread_a = spread(w_full, base_a + x * a1, a1, nx, x_peer)

    arrive(h_y)
    arrive(h_z)
    rhx[pl.ds(x, 1)] = (summed_slots(rhy, ny) + summed_slots(rhz, nz)).astype(BF)[None]
    h_x = share(rhx, x, nx, x_peer)

    arrive(g_z)
    g_mine = pl.multiple_of(xc * gx, 16)
    gfull[pl.ds(g_mine, gx), :] = summed_slots(rgz, nz).astype(BF)
    g_xs = spread(gfull, g_mine, gx, nx * nc, xc_peer)

    settle(fourth_count)

    def field_of(start, stop):
        at, weights = slice(start, stop), w_full[start:stop, :]
        return nn(cosine[:, at], weights), nn(sine[:, at], weights)

    arrive(spread_b)
    arrive(spread_c)
    of_cos, of_sin = field_of(base_b, K)
    arrive(spread_a)
    more_cos, more_sin = field_of(base_a, base_b)
    field = of_cos + more_cos + pltpu.roll(of_sin + more_sin, 64, 1)
    e_out[...] = field[A:, :].astype(BF)
    e_swap = [send(e_out, e_in, sibling)]
    field_here = field[:A, :]

    arrive(h_x)
    h2[...] = summed_slots(rhx, nx).astype(BF)
    h_swap = [send(h2, h_in, sibling)]

    arrive(e_swap)
    here = field_here.astype(BF).astype(F32)
    there = e_in[...].astype(F32)
    potential = by_core(here, there).astype(BF)[:, :64]
    grad_charge = by_core(there, here).astype(BF)[:, :64]
    out[0:A, :] = alive * (short_range + nn(potential, fw[...]))
    out[A : 2 * A, :] = alive * (short_grad + nn(grad_charge, cw[...]))

    arrive(h_swap)
    here, there = h2[...].astype(F32), h_in[...].astype(F32)
    out[6 * C : 6 * C + 64, :] = by_core(here, there) * grad_scale
    out[6 * C + 64 : 7 * C, :] = by_core(there, here) * grad_scale

    arrive(g_xs)
    out[2 * C : 6 * C, :] = gfull[...].astype(F32) * grad_scale

    settle(len(sent))


def place(
    rows, o_layer, o_feat, o_sg, o_tg, o_eg, o_mg, o_cg, o_fg, layer, feat, sem
):
    layer[...] = rows[0:A, :].astype(BF)
    feat[...] = rows[A : 2 * A, :].astype(BF)
    moves = [(layer, o_layer), (feat, o_feat)]
    moves += [
        (rows.at[pl.ds((i + 2) * C, C)], out) for i, out in enumerate((o_sg, o_tg, o_eg, o_mg))
    ]
    moves += [(rows.at[pl.ds(6 * C, 64)], o_cg), (rows.at[pl.ds(6 * C + 64, 64)], o_fg)]
    copies = [pltpu.make_async_copy(a, b, sem.at[i]) for i, (a, b) in enumerate(moves)]
    for copy in copies:
        copy.start()
    for copy in copies:
        copy.wait()


def local(
    features, positions, neighbours, distances, ghost_rows, atom_counts, wavevectors,
    wave_weights, source_weight, target_weight, edge_weight, mix_weight, charge_weight,
    field_weight, cotangent,
):
    geo = GEOMETRY
    nx, ny, nc, nz = geo["x"], geo["y"], geo["core"], geo["z_lo"] * geo["z_hi"]
    total_atoms = A * lax.axis_size("dx") * lax.axis_size("dy")
    factor_scale = 4.0 / math.sqrt(total_atoms * K)
    grad_scale = 1.0 / math.sqrt(total_atoms)
    a1, b1, c1 = ROWS[0] // nx, ROWS[1] // ny, ROWS[2] // nz
    a2, b2, c2 = a1 // ny, b1 // nx, c1 // nx
    last = a2 + b2 + c2
    gx = 4 * C // (nx * nc)

    def bf(*shape):
        return pltpu.VMEM(shape, BF)

    def f32(*shape):
        return pltpu.VMEM(shape, F32)

    scratch = [
        bf(A, C), bf(A, C), f32(8, A), f32(8, A), f32(8, K), bf(K, 2 * C),
        bf(nx - 1, a1, 2 * C), bf(a1, 2 * C),
        bf(ny - 1, b1, 2 * C), bf(b1, 2 * C),
        bf(nz - 1, c1, 2 * C), bf(c1, 2 * C),
        bf(ny - 1, a2, 2 * C), bf(nx - 1, b2, 2 * C), bf(nx - 1, c2, 2 * C),
        bf(last, 2 * C), bf(nz, a2 + b2, 2 * C), bf(ny, c2, 2 * C), bf(last, 2 * C),
        bf(last, C), bf(last, C), bf(K, C), bf(2 * A, K), bf(2 * A, K), bf(A, C), bf(A, C),
        bf(A, C), bf(A, C), bf(A, C), bf(A, C),
        bf(4 * C, C), bf(nx * nc - 1, gx, C), bf(gx, C), bf(ny, gx, C), bf(nz, gx, C),
        bf(4 * C, C),
        bf(ny, 64, C), bf(nz, 64, C), bf(nx, 64, C), bf(64, C), bf(64, C),
        bf(2 * A, STEP * A), bf(C, STEP * A), f32(C, STEP * A),
        bf(C, STEP * A), bf(C, STEP * A),
        f32(NB, A), f32(NB, A), f32(C, A), f32(C, A), bf(C, 2 * A), f32(A, A),
        f32(C, A), f32(C, A), f32(2 * A, C), f32(C, C),
        pltpu.SemaphoreType.DMA((COPIES,)),
        pltpu.SemaphoreType.DMA((COPIES,)),
    ]
    vmem = pl.BlockSpec(memory_space=pltpu.VMEM)
    anywhere = pl.BlockSpec(memory_space=pl.ANY)
    operands = (
        features, positions, neighbours.T, distances.T, ghost_rows, atom_counts, wavevectors,
        wave_weights.reshape(1, K), source_weight, target_weight, edge_weight, mix_weight,
        charge_weight.T, field_weight, cotangent,
    )
    n_in = len(operands)
    held = [
        pltpu.SMEM(a.shape, a.dtype) if a.ndim == 1 else pltpu.VMEM(a.shape, a.dtype)
        for a in operands
    ]

    def kernel(*refs):
        left = refs[n_in + 1 :]
        body(factor_scale, grad_scale, refs[:n_in], refs[n_in], left[:n_in], *left[n_in:])

    rows = pl.pallas_call(
        kernel,
        out_shape=jax.ShapeDtypeStruct((7 * C, C), F32),
        in_specs=[anywhere] * n_in,
        out_specs=vmem,
        scratch_shapes=held + [pltpu.SemaphoreType.DMA((n_in,))] + scratch,
        compiler_params=pltpu.CompilerParams(
            collective_id=0, has_side_effects=True, vmem_limit_bytes=60 * 1024 * 1024
        ),
        name="ewald_layer",
    )(*operands)
    outs = pl.pallas_call(
        place,
        out_shape=[jax.ShapeDtypeStruct((A, C), BF)] * 2
        + [jax.ShapeDtypeStruct((C, C), F32)] * 4
        + [jax.ShapeDtypeStruct((64, C), F32)] * 2,
        in_specs=[vmem],
        out_specs=[anywhere] * 8,
        scratch_shapes=[bf(A, C), bf(A, C), pltpu.SemaphoreType.DMA((8,))],
        name="place_outputs",
    )(rows)
    return (*outs[:6], outs[6].T, outs[7])


def solution(mesh):
    atoms = P(("dx", "dy"), None)
    in_specs = (
        atoms, P(None, ("dx", "dy")), atoms, atoms, P(None, ("dx", "dy")), P(("dx", "dy")),
        P(), P(), P(), P(), P(), P(), P(), P(), atoms,
    )
    out_specs = (atoms, atoms, P(), P(), P(), P(), P(), P())
    return jax.shard_map(
        local, mesh=mesh, in_specs=in_specs, out_specs=out_specs, check_vma=False
    )
```

```python
import math

import jax
import jax.numpy as jnp
from jax import lax
from jax.experimental import pallas as pl
from jax.experimental.pallas import tpu as pltpu
from jax.sharding import PartitionSpec as P

GEOMETRY = dict(y=8, z_hi=4, x=4, z_lo=2, core=2)
K = 2048
C = 128
A = 128
NB = 64
STEP = 16
COPIES = 140
ROWS = (1024, 512, 512)

FIRST = (0, 14, 4, 5, 1, 6, 7)
LATER = (2, 3, 8, 9, 10, 11, 12, 13)

BF = jnp.bfloat16
F32 = jnp.float32


def nn(a, b):
    return lax.dot_general(a, b, (((1,), (0,)), ((), ())), preferred_element_type=F32)


def nt(a, b):
    return lax.dot_general(a, b, (((1,), (1,)), ((), ())), preferred_element_type=F32)


def half_turns(f):
    q = f * f
    s = 0.10982452
    for c in (-0.84611165, 3.60635422, -7.30824569, 4.44288292):
        s = s * q + c
    c0 = 0.31068803
    for c in (-1.88355791, 5.73946038, -6.97885095, 1.4142135):
        c0 = c0 * q + c
    return s * f, c0


def body(
    factor_scale,
    grad_scale,
    operands,
    out,
    held, held_sem,
    x_out, x_in, pos_out, pos_in, kv, sums,
    la, ta, lb, tb, lc, tc, la2, lb2, lc2, t2, lz, ly, fin,
    w_out, w_in, w_full, cosine, sine, e_out, e_in,
    gout, gin, ggout, gret,
    g0, rgx, g1, rgy, rgz, gfull,
    rhy, rhz, rhx, h2, h_in,
    picks, hiddens, slopes, inners, pairs,
    nbr_t, gate_t, src_t, ga_t, tab_t, pick_t, agg_t, gs_t, tsum, epart,
    ssem, rsem,
):
    fetch = [
        pltpu.make_async_copy(src, dst, held_sem.at[i])
        for i, (src, dst) in enumerate(zip(operands, held))
    ]
    for i in FIRST + LATER:
        fetch[i].start()
    feat, pos, nbr, dist, ghost, counts, kvec, kw, sw, tw, ew, mw, cw, fw, cot = held

    geo = GEOMETRY
    nx, ny, nc = geo["x"], geo["y"], geo["core"]
    nzl, nzh = geo["z_lo"], geo["z_hi"]
    nz = nzl * nzh
    ndx, ndy = ny * nzh * nx, nzl * nc
    dx, dy = lax.axis_index("dx"), lax.axis_index("dy")
    x = lax.rem(dx, nx)
    zh = lax.rem(lax.div(dx, nx), nzh)
    y = lax.div(dx, nx * nzh)
    zl, core = lax.div(dy, nc), lax.rem(dy, nc)
    z = zh * nzl + zl

    def device(px=None, py=None, pz=None, pc=None):
        px = x if px is None else px
        py = y if py is None else py
        pz = z if pz is None else pz
        pc = core if pc is None else pc
        return (
            (py * nzh + lax.div(pz, nzl)) * nx + px,
            lax.rem(pz, nzl) * nc + pc,
        )

    def ahead(me, d, n):
        return lax.rem(me + d, n)

    def x_peer(d):
        return device(px=ahead(x, d, nx))

    def y_peer(d):
        return device(py=ahead(y, d, ny))

    def z_peer(d):
        return device(pz=ahead(z, d, nz))

    def xc_peer(d):
        return device(px=ahead(x, d // nc, nx), pc=ahead(core, d % nc, nc))

    sibling = device(pc=ahead(core, 1, nc))
    faces = (
        (ahead(dx, 1, ndx), dy),
        (ahead(dx, ndx - 1, ndx), dy),
        (dx, ahead(dy, 1, ndy)),
        (dx, ahead(dy, ndy - 1, ndy)),
    )
    back = (faces[1], faces[0], faces[3], faces[2])

    barrier = pltpu.get_barrier_semaphore()
    greeted = list(faces)
    greeted += [xc_peer(d) for d in range(1, nx * nc)]
    greeted += [y_peer(d) for d in range(1, ny)]
    greeted += [z_peer(d) for d in range(1, nz)]
    for other in greeted:
        pl.semaphore_signal(
            barrier, inc=1, device_id=other, device_id_type=pl.DeviceIdType.MESH
        )

    sent = []

    def send(src, dst, other):
        slot = len(sent)
        copy = pltpu.make_async_remote_copy(
            src_ref=src,
            dst_ref=dst,
            send_sem=ssem.at[slot],
            recv_sem=rsem.at[slot],
            device_id=other,
            device_id_type=pl.DeviceIdType.MESH,
        )
        copy.start()
        sent.append(copy)
        return copy

    def arrive(copies):
        for copy in copies:
            copy.wait_recv()

    settled = []

    def settle(upto):
        for copy in sent[len(settled) : upto]:
            copy.wait_send()
            settled.append(copy)

    def far_first(n):
        return sorted(range(1, n), key=lambda d: -min(d, n - d))

    def rows(ref, start, size):
        return ref.at[pl.ds(pl.multiple_of(start, 16), size)]

    def scatter(src, base, landing, me, n, size, peer):
        return [
            send(rows(src, base + ahead(me, d, n) * size, size), landing.at[d - 1], peer(d))
            for d in far_first(n)
        ]

    def collect(src, base, landing, me, n, size, dst, dst_base=0):
        chunk = min(size, 128)

        def add(i, _):
            at = pl.multiple_of(i * chunk, 16)
            total = src[pl.ds(pl.multiple_of(base + me * size + at, 16), chunk), :].astype(F32)
            for d in range(1, n):
                total += landing[d - 1, pl.ds(at, chunk), :].astype(F32)
            dst[pl.ds(pl.multiple_of(dst_base + at, 16), chunk), :] = total.astype(BF)
            return 0

        if size == chunk:
            add(0, 0)
        else:
            lax.fori_loop(0, size // chunk, add, 0)

    def share(landing, me, n, peer):
        return [send(landing.at[me], landing.at[me], peer(d)) for d in far_first(n)]

    def summed_slots(landing, n):
        total = landing[0].astype(F32)
        for d in range(1, n):
            total += landing[d].astype(F32)
        return total

    def spread(ref, start, size, n, peer):
        return [
            send(rows(ref, start, size), rows(ref, start, size), peer(d)) for d in far_first(n)
        ]

    first_core = jnp.where(core == 0, 1.0, 0.0).astype(F32)

    def by_core(mine_if_first, mine_if_second):
        return first_core * mine_if_first + (1.0 - first_core) * mine_if_second

    for i in FIRST:
        fetch[i].wait()

    row_id = lax.broadcasted_iota(jnp.int32, (A, C), 0)
    alive = jnp.where(row_id < counts[0], 1.0, 0.0).astype(F32)
    masked32 = feat[...].astype(F32) * alive
    gm32 = cot[...].astype(F32) * alive
    masked, gm = masked32.astype(BF), gm32.astype(BF)
    for f in range(4):
        pick_t[:, f * 32 : (f + 1) * 32] = jnp.where(
            lax.broadcasted_iota(jnp.int32, (A, 32), 0) == ghost[f : f + 1, :], 1.0, 0.0
        )
    gout[...] = nn(pick_t[...].T.astype(BF), masked).astype(BF)
    x_out[...] = by_core(gm32, masked32).astype(BF)
    pos_out[...] = jnp.zeros_like(pos_out)
    pos_out[0:3, :] = pos[...]

    own_kind = by_core(masked32, gm32).astype(BF)
    kv[...] = jnp.zeros_like(kv)
    kv[0:3, :] = kvec[...] * (1.0 / (2.0 * math.pi))
    kv[3:4, :] = jnp.sqrt(kw[...] * factor_scale)

    def waves(turns, root):
        s, c = half_turns(turns - jnp.round(turns))
        s_root = s * root
        return (root - s * s_root).astype(BF), (c * s_root).astype(BF)

    def add_waves(first_row, place, start, stop):
        spots = [jnp.broadcast_to(place[a : a + 1, :], (A, A)).T for a in range(3)]
        spots = [jnp.concatenate([spot, spot], axis=1) for spot in spots]
        atoms = slice(first_row, first_row + A)

        def wave_block(block, _):
            at = pl.ds(pl.multiple_of(block * 256, 256), 256)
            turns = spots[0] * kv[0:1, at] + spots[1] * kv[1:2, at] + spots[2] * kv[2:3, at]
            cosine[atoms, at], sine[atoms, at] = waves(turns, kv[3:4, at])
            return 0

        lax.fori_loop(start // 256, stop // 256, wave_block, 0)

    add_waves(0, pos_out, 0, K)
    own_t = own_kind.astype(F32).T

    for i in LATER:
        fetch[i].wait()

    masked_t = masked32.T.astype(BF)

    src_t[...] = nn(masked, sw[...]).astype(BF).astype(F32).T
    ga_t[...] = nt(gm, mw[...]).astype(BF).astype(F32).T
    nbr_t[...] = nbr[...].astype(F32)
    s, c = half_turns(dist[...] * 0.1)
    gate_t[...] = jnp.where(nbr[...] < 2 * A, 0.5 * c * c, 0.0)
    tab_t[:, :A] = nn(masked, tw[...]).astype(BF).astype(F32).T.astype(BF)
    agg_t[...] = jnp.zeros_like(agg_t)
    gs_t[...] = jnp.zeros_like(gs_t)
    tsum[...] = jnp.zeros_like(tsum)
    epart[...] = jnp.zeros_like(epart)
    ew_t = ew[...].astype(F32).T.astype(BF)

    pl.semaphore_wait(barrier, len(greeted))
    atoms_in = [send(x_out, x_in, sibling), send(pos_out, pos_in, sibling)]
    ghosts_in = [
        send(gout.at[pl.ds(f * 32, 32)], gin.at[pl.ds(f * 32, 32)], faces[f]) for f in range(4)
    ]
    arrive(atoms_in)

    values_t = jnp.concatenate([own_t, x_in[...].astype(F32).T], axis=1).astype(BF)

    def sum_block(block, _):
        at = pl.ds(pl.multiple_of(block * 512, 512), 512)
        of_cos = nn(values_t, cosine[:, at]).astype(BF)
        of_sin = nn(values_t, sine[:, at]).astype(BF)
        sums[at, :C] = of_cos.T
        sums[at, C:] = of_sin.T
        return 0

    def add_sums(start, stop):
        add_waves(A, pos_in, start, stop)
        lax.fori_loop(start // 512, stop // 512, sum_block, 0)

    base_a, base_b, base_c = 0, ROWS[0], ROWS[0] + ROWS[1]
    a1, b1, c1 = ROWS[0] // nx, ROWS[1] // ny, ROWS[2] // nz
    a2, b2, c2 = a1 // ny, b1 // nx, c1 // nx
    add_sums(0, base_b)
    first_a = scatter(sums, base_a, la, x, nx, a1, x_peer)
    add_sums(base_b, base_c)
    first_b = scatter(sums, base_b, lb, y, ny, b1, y_peer)
    add_sums(base_c, K)
    first_c = scatter(sums, base_c, lc, z, nz, c1, z_peer)

    table_row = lax.broadcasted_iota(jnp.int32, (2 * A, A), 0).astype(F32).astype(BF)

    arrive(ghosts_in)
    ghosts = gin[...]
    tab_t[:, A:] = nn(ghosts, tw[...]).astype(BF).astype(F32).T.astype(BF)
    table_t = jnp.concatenate([masked_t, ghosts.astype(F32).T.astype(BF)], axis=1)

    def edge_step(step, _):
        slots = [(pl.ds(step * STEP + j, 1), slice(j * A, (j + 1) * A)) for j in range(STEP)]
        for row, at in slots:
            named = jnp.broadcast_to(nbr_t[row, :], (2 * A, A)).astype(BF)
            picks[:, at] = jnp.where(table_row == named, jnp.ones((), BF), jnp.zeros((), BF))
        summed = nn(tab_t[...], picks[...])
        for row, at in slots:
            v = summed[:, at] + src_t[...]
            g = 0.5 * jnp.tanh(0.5 * v) + 0.5
            hidden = v * g
            hiddens[:, at] = hidden.astype(BF)
            slopes[:, at] = g + hidden * (1.0 - g)
        mixed = nn(ew_t, hiddens[...])
        agg_sum = agg_t[...]
        for row, at in slots:
            v = mixed[:, at]
            g = 0.5 * jnp.tanh(0.5 * v) + 0.5
            message = v * g
            agg_sum += gate_t[row, :] * message
            inners[:, at] = (gate_t[row, :] * ga_t[...] * (g + message * (1.0 - g))).astype(BF)
        agg_t[...] = agg_sum
        outer = nn(ew[...], inners[...])
        gs_sum = gs_t[...]
        for row, at in slots:
            pair_grad = outer[:, at] * slopes[:, at]
            gs_sum += pair_grad
            pairs[:, at] = pair_grad.astype(BF)
        gs_t[...] = gs_sum
        epart[...] += nt(hiddens[...], inners[...])
        tsum[...] += nt(picks[...], pairs[...])
        return 0

    steps = NB // STEP
    lax.fori_loop(0, steps - 1, edge_step, 0)
    first_count = len(sent)
    arrive(first_a)
    collect(sums, base_a, la, x, nx, a1, ta)
    second_a = scatter(ta, 0, la2, y, ny, a2, y_peer)
    arrive(first_b)
    collect(sums, base_b, lb, y, ny, b1, tb)
    second_b = scatter(tb, 0, lb2, x, nx, b2, x_peer)
    arrive(first_c)
    collect(sums, base_c, lc, z, nz, c1, tc)
    second_c = scatter(tc, 0, lc2, x, nx, c2, x_peer)

    lax.fori_loop(steps - 1, steps, edge_step, 0)
    table_sum = tsum[...]
    aggregate_t = agg_t[...].astype(BF)
    grad_source = gs_t[...].T.astype(BF)
    g0[0:C, :] = nn(masked_t, grad_source).astype(BF)
    g0[C : 2 * C, :] = nn(table_t, table_sum.astype(BF)).astype(BF)
    g0[2 * C : 3 * C, :] = epart[...].astype(BF)
    g0[3 * C :, :] = nn(aggregate_t, gm).astype(BF)
    gx = 4 * C // (nx * nc)
    xc = x * nc + core
    g_x = [
        send(
            rows(g0, (ahead(x, d // nc, nx) * nc + ahead(core, d % nc, nc)) * gx, gx),
            rgx.at[d - 1],
            xc_peer(d),
        )
        for d in range(1, nx * nc)
    ]

    ggout[...] = table_sum[A:, :].astype(BF)
    ghosts_back = [
        send(ggout.at[pl.ds(f * 32, 32)], gret.at[pl.ds(f * 32, 32)], back[f]) for f in range(4)
    ]
    second_count = len(sent)
    ab2 = a2 + b2
    settle(first_count)
    arrive(second_b)
    collect(tb, 0, lb2, x, nx, b2, t2, a2)
    arrive(second_c)
    collect(tc, 0, lc2, x, nx, c2, t2, ab2)
    ly[pl.ds(y, 1)] = t2[ab2:, :][None]
    third_c = share(ly, y, ny, y_peer)
    arrive(second_a)
    collect(ta, 0, la2, y, ny, a2, t2, 0)
    lz[pl.ds(z, 1)] = t2[:ab2, :][None]
    third_ab = share(lz, z, nz, z_peer)

    arrive(g_x)
    collect(g0, 0, rgx, xc, nx * nc, gx, g1)
    rgy[pl.ds(y, 1)] = g1[...][None]
    g_y = share(rgy, y, ny, y_peer)

    arrive(ghosts_back)
    grad_target = (table_sum[:A, :] + nn(pick_t[...].astype(BF), gret[...])).astype(BF)
    short_grad = nt(grad_source, sw[...]) + nt(grad_target, tw[...])
    short_range = nn(agg_t[...].T.astype(BF), mw[...])

    fw_t = fw[...].astype(F32).T
    project = by_core(cw[...].astype(F32).T, fw_t).astype(BF)
    none = jnp.zeros((C, 64), BF)
    project = jnp.concatenate(
        [
            jnp.concatenate([project, none], axis=1),
            jnp.concatenate([none, project], axis=1),
        ],
        axis=0,
    )
    third_count = len(sent)
    settle(second_count)
    arrive(third_c)
    fin[ab2:, :] = summed_slots(ly, ny).astype(BF)
    arrive(third_ab)
    fin[:ab2, :] = summed_slots(lz, nz).astype(BF)
    w_out[...] = nn(fin[...], project).astype(BF)
    w_swap = [send(w_out, w_in, sibling)]
    place_a = pl.multiple_of(base_a + x * a1 + y * a2, 16)
    place_b = pl.multiple_of(base_b + y * b1 + x * b2, 16)
    place_c = pl.multiple_of(base_c + z * c1 + x * c2, 16)
    w_full[pl.ds(place_a, a2), :] = w_out[:a2, :]
    w_full[pl.ds(place_b, b2), :] = w_out[a2:ab2, :]
    w_full[pl.ds(place_c, c2), :] = w_out[ab2:, :]
    spread_a = spread(w_full, place_a, a2, ny, y_peer)
    spread_b = spread(w_full, place_b, b2, nx, x_peer)
    spread_c = spread(w_full, place_c, c2, nx, x_peer)

    arrive(w_swap)
    other_t = w_in[...].astype(F32).T
    in_ab = lax.broadcasted_iota(jnp.int32, other_t.shape, 1) < ab2

    def weight_part(left):
        quads = nn(left.astype(BF), fin[...])
        return (quads[:64, :C] + quads[64:, C:]).astype(BF)

    rhy[pl.ds(y, 1)] = weight_part(jnp.where(in_ab, other_t, 0.0))[None]
    rhz[pl.ds(z, 1)] = weight_part(jnp.where(in_ab, 0.0, other_t))[None]

    h_y = share(rhy, y, ny, y_peer)
    h_z = share(rhz, z, nz, z_peer)

    arrive(g_y)
    rgz[pl.ds(z, 1)] = summed_slots(rgy, ny).astype(BF)[None]
    g_z = share(rgz, z, nz, z_peer)

    settle(third_count)
    fourth_count = len(sent)
    arrive(spread_b)
    spread_b = spread(w_full, base_b + y * b1, b1, ny, y_peer)
    arrive(spread_c)
    spread_c = spread(w_full, base_c + z * c1, c1, nz, z_peer)
    arrive(spread_a)
    spread_a = spread(w_full, base_a + x * a1, a1, nx, x_peer)

    arrive(h_y)
    arrive(h_z)
    rhx[pl.ds(x, 1)] = (summed_slots(rhy, ny) + summed_slots(rhz, nz)).astype(BF)[None]
    h_x = share(rhx, x, nx, x_peer)

    arrive(g_z)
    g_mine = pl.multiple_of(xc * gx, 16)
    gfull[pl.ds(g_mine, gx), :] = summed_slots(rgz, nz).astype(BF)
    g_xs = spread(gfull, g_mine, gx, nx * nc, xc_peer)

    settle(fourth_count)

    def field_of(start, stop):
        at, weights = slice(start, stop), w_full[start:stop, :]
        return nn(cosine[:, at], weights), nn(sine[:, at], weights)

    arrive(spread_b)
    arrive(spread_c)
    of_cos, of_sin = field_of(base_b, K)
    arrive(spread_a)
    more_cos, more_sin = field_of(base_a, base_b)
    field = of_cos + more_cos + pltpu.roll(of_sin + more_sin, 64, 1)
    e_out[...] = field[A:, :].astype(BF)
    e_swap = [send(e_out, e_in, sibling)]
    field_here = field[:A, :]

    arrive(h_x)
    h2[...] = summed_slots(rhx, nx).astype(BF)
    h_swap = [send(h2, h_in, sibling)]

    arrive(e_swap)
    here = field_here.astype(BF).astype(F32)
    there = e_in[...].astype(F32)
    potential = by_core(here, there).astype(BF)[:, :64]
    grad_charge = by_core(there, here).astype(BF)[:, :64]
    out[0:A, :] = alive * (short_range + nn(potential, fw[...]))
    out[A : 2 * A, :] = alive * (short_grad + nn(grad_charge, cw[...]))

    arrive(h_swap)
    here, there = h2[...].astype(F32), h_in[...].astype(F32)
    out[6 * C : 6 * C + 64, :] = by_core(here, there) * grad_scale
    out[6 * C + 64 : 7 * C, :] = by_core(there, here) * grad_scale

    arrive(g_xs)
    out[2 * C : 6 * C, :] = gfull[...].astype(F32) * grad_scale

    settle(len(sent))


def place(
    rows, o_layer, o_feat, o_sg, o_tg, o_eg, o_mg, o_cg, o_fg, layer, feat, sem
):
    layer[...] = rows[0:A, :].astype(BF)
    feat[...] = rows[A : 2 * A, :].astype(BF)
    moves = [(layer, o_layer), (feat, o_feat)]
    moves += [
        (rows.at[pl.ds((i + 2) * C, C)], out) for i, out in enumerate((o_sg, o_tg, o_eg, o_mg))
    ]
    moves += [(rows.at[pl.ds(6 * C, 64)], o_cg), (rows.at[pl.ds(6 * C + 64, 64)], o_fg)]
    copies = [pltpu.make_async_copy(a, b, sem.at[i]) for i, (a, b) in enumerate(moves)]
    for copy in copies:
        copy.start()
    for copy in copies:
        copy.wait()


def local(
    features, positions, neighbours, distances, ghost_rows, atom_counts, wavevectors,
    wave_weights, source_weight, target_weight, edge_weight, mix_weight, charge_weight,
    field_weight, cotangent,
):
    geo = GEOMETRY
    nx, ny, nc, nz = geo["x"], geo["y"], geo["core"], geo["z_lo"] * geo["z_hi"]
    total_atoms = A * lax.axis_size("dx") * lax.axis_size("dy")
    factor_scale = 4.0 / math.sqrt(total_atoms * K)
    grad_scale = 1.0 / math.sqrt(total_atoms)
    a1, b1, c1 = ROWS[0] // nx, ROWS[1] // ny, ROWS[2] // nz
    a2, b2, c2 = a1 // ny, b1 // nx, c1 // nx
    last = a2 + b2 + c2
    gx = 4 * C // (nx * nc)

    def bf(*shape):
        return pltpu.VMEM(shape, BF)

    def f32(*shape):
        return pltpu.VMEM(shape, F32)

    scratch = [
        bf(A, C), bf(A, C), f32(8, A), f32(8, A), f32(8, K), bf(K, 2 * C),
        bf(nx - 1, a1, 2 * C), bf(a1, 2 * C),
        bf(ny - 1, b1, 2 * C), bf(b1, 2 * C),
        bf(nz - 1, c1, 2 * C), bf(c1, 2 * C),
        bf(ny - 1, a2, 2 * C), bf(nx - 1, b2, 2 * C), bf(nx - 1, c2, 2 * C),
        bf(last, 2 * C), bf(nz, a2 + b2, 2 * C), bf(ny, c2, 2 * C), bf(last, 2 * C),
        bf(last, C), bf(last, C), bf(K, C), bf(2 * A, K), bf(2 * A, K), bf(A, C), bf(A, C),
        bf(A, C), bf(A, C), bf(A, C), bf(A, C),
        bf(4 * C, C), bf(nx * nc - 1, gx, C), bf(gx, C), bf(ny, gx, C), bf(nz, gx, C),
        bf(4 * C, C),
        bf(ny, 64, C), bf(nz, 64, C), bf(nx, 64, C), bf(64, C), bf(64, C),
        bf(2 * A, STEP * A), bf(C, STEP * A), f32(C, STEP * A),
        bf(C, STEP * A), bf(C, STEP * A),
        f32(NB, A), f32(NB, A), f32(C, A), f32(C, A), bf(C, 2 * A), f32(A, A),
        f32(C, A), f32(C, A), f32(2 * A, C), f32(C, C),
        pltpu.SemaphoreType.DMA((COPIES,)),
        pltpu.SemaphoreType.DMA((COPIES,)),
    ]
    vmem = pl.BlockSpec(memory_space=pltpu.VMEM)
    anywhere = pl.BlockSpec(memory_space=pl.ANY)
    operands = (
        features, positions, neighbours.T, distances.T, ghost_rows, atom_counts, wavevectors,
        wave_weights.reshape(1, K), source_weight, target_weight, edge_weight, mix_weight,
        charge_weight.T, field_weight, cotangent,
    )
    n_in = len(operands)
    held = [
        pltpu.SMEM(a.shape, a.dtype) if a.ndim == 1 else pltpu.VMEM(a.shape, a.dtype)
        for a in operands
    ]

    def kernel(*refs):
        left = refs[n_in + 1 :]
        body(factor_scale, grad_scale, refs[:n_in], refs[n_in], left[:n_in], *left[n_in:])

    rows = pl.pallas_call(
        kernel,
        out_shape=jax.ShapeDtypeStruct((7 * C, C), F32),
        in_specs=[anywhere] * n_in,
        out_specs=vmem,
        scratch_shapes=held + [pltpu.SemaphoreType.DMA((n_in,))] + scratch,
        compiler_params=pltpu.CompilerParams(
            collective_id=0, has_side_effects=True, vmem_limit_bytes=60 * 1024 * 1024
        ),
        name="ewald_layer",
    )(*operands)
    outs = pl.pallas_call(
        place,
        out_shape=[jax.ShapeDtypeStruct((A, C), BF)] * 2
        + [jax.ShapeDtypeStruct((C, C), F32)] * 4
        + [jax.ShapeDtypeStruct((64, C), F32)] * 2,
        in_specs=[vmem],
        out_specs=[anywhere] * 8,
        scratch_shapes=[bf(A, C), bf(A, C), pltpu.SemaphoreType.DMA((8,))],
        name="place_outputs",
    )(rows)
    return (*outs[:6], outs[6].T, outs[7])


def solution(mesh):
    atoms = P(("dx", "dy"), None)
    in_specs = (
        atoms, P(None, ("dx", "dy")), atoms, atoms, P(None, ("dx", "dy")), P(("dx", "dy")),
        P(), P(), P(), P(), P(), P(), P(), P(), atoms,
    )
    out_specs = (atoms, atoms, P(), P(), P(), P(), P(), P())
    return jax.shard_map(
        local, mesh=mesh, in_specs=in_specs, out_specs=out_specs, check_vma=False
    )
```

```python
import math

import jax
import jax.numpy as jnp
from jax import lax
from jax.experimental import pallas as pl
from jax.experimental.pallas import tpu as pltpu
from jax.sharding import PartitionSpec as P

GEOMETRY = dict(y=8, z_hi=4, x=4, z_lo=2, core=2)
K = 2048
C = 128
A = 128
NB = 64
STEP = 16
COPIES = 140
ROWS = (1024, 512, 512)

FIRST = (0, 14, 4, 5, 1, 6, 7)
LATER = (2, 3, 8, 9, 10, 11, 12, 13)

BF = jnp.bfloat16
F32 = jnp.float32


def nn(a, b):
    return lax.dot_general(a, b, (((1,), (0,)), ((), ())), preferred_element_type=F32)


def nt(a, b):
    return lax.dot_general(a, b, (((1,), (1,)), ((), ())), preferred_element_type=F32)


def half_turns(f):
    q = f * f
    s = 0.10982452
    for c in (-0.84611165, 3.60635422, -7.30824569, 4.44288292):
        s = s * q + c
    c0 = 0.31068803
    for c in (-1.88355791, 5.73946038, -6.97885095, 1.4142135):
        c0 = c0 * q + c
    return s * f, c0


def body(
    factor_scale,
    grad_scale,
    operands,
    out,
    held, held_sem,
    x_out, x_in, pos_out, pos_in, kv, sums,
    la, ta, lb, tb, lc, tc, la2, lb2, lc2, t2, lz, ly, fin,
    w_out, w_in, w_full, cosine, sine, e_out, e_in,
    gout, gin, ggout, gret,
    g0, rgx, g1, rgy, rgz, gfull,
    rhy, rhz, rhx, h2, h_in,
    picks, hiddens, slopes, inners, pairs,
    nbr_t, gate_t, src_t, ga_t, tab_t, pick_t, agg_t, gs_t, tsum, epart,
    ssem, rsem,
):
    fetch = [
        pltpu.make_async_copy(src, dst, held_sem.at[i])
        for i, (src, dst) in enumerate(zip(operands, held))
    ]
    for i in FIRST + LATER:
        fetch[i].start()
    feat, pos, nbr, dist, ghost, counts, kvec, kw, sw, tw, ew, mw, cw, fw, cot = held

    geo = GEOMETRY
    nx, ny, nc = geo["x"], geo["y"], geo["core"]
    nzl, nzh = geo["z_lo"], geo["z_hi"]
    nz = nzl * nzh
    ndx, ndy = ny * nzh * nx, nzl * nc
    dx, dy = lax.axis_index("dx"), lax.axis_index("dy")
    x = lax.rem(dx, nx)
    zh = lax.rem(lax.div(dx, nx), nzh)
    y = lax.div(dx, nx * nzh)
    zl, core = lax.div(dy, nc), lax.rem(dy, nc)
    z = zh * nzl + zl

    def device(px=None, py=None, pz=None, pc=None):
        px = x if px is None else px
        py = y if py is None else py
        pz = z if pz is None else pz
        pc = core if pc is None else pc
        return (
            (py * nzh + lax.div(pz, nzl)) * nx + px,
            lax.rem(pz, nzl) * nc + pc,
        )

    def ahead(me, d, n):
        return lax.rem(me + d, n)

    def x_peer(d):
        return device(px=ahead(x, d, nx))

    def y_peer(d):
        return device(py=ahead(y, d, ny))

    def z_peer(d):
        return device(pz=ahead(z, d, nz))

    def xc_peer(d):
        return device(px=ahead(x, d // nc, nx), pc=ahead(core, d % nc, nc))

    sibling = device(pc=ahead(core, 1, nc))
    faces = (
        (ahead(dx, 1, ndx), dy),
        (ahead(dx, ndx - 1, ndx), dy),
        (dx, ahead(dy, 1, ndy)),
        (dx, ahead(dy, ndy - 1, ndy)),
    )
    back = (faces[1], faces[0], faces[3], faces[2])

    barrier = pltpu.get_barrier_semaphore()
    def far_first(n):
        return sorted(range(1, n), key=lambda d: -min(d, n - d))

    greeted = []
    for in_y, in_z in zip(far_first(ny), far_first(nz)):
        greeted += [y_peer(in_y), z_peer(in_z)]
    greeted = greeted[:6] + list(faces) + greeted[6:]
    greeted += [xc_peer(d) for d in far_first(nx * nc)]
    for other in greeted:
        pl.semaphore_signal(
            barrier, inc=1, device_id=other, device_id_type=pl.DeviceIdType.MESH
        )

    sent = []

    def send(src, dst, other):
        slot = len(sent)
        copy = pltpu.make_async_remote_copy(
            src_ref=src,
            dst_ref=dst,
            send_sem=ssem.at[slot],
            recv_sem=rsem.at[slot],
            device_id=other,
            device_id_type=pl.DeviceIdType.MESH,
        )
        copy.start()
        sent.append(copy)
        return copy

    def arrive(copies):
        for copy in copies:
            copy.wait_recv()

    settled = []

    def settle(upto):
        for copy in sent[len(settled) : upto]:
            copy.wait_send()
            settled.append(copy)

    def rows(ref, start, size):
        return ref.at[pl.ds(pl.multiple_of(start, 16), size)]

    def scatter(src, base, landing, me, n, size, peer):
        return [
            send(rows(src, base + ahead(me, d, n) * size, size), landing.at[d - 1], peer(d))
            for d in far_first(n)
        ]

    def collect(src, base, landing, me, n, size, dst, dst_base=0):
        chunk = min(size, 128)

        def add(i, _):
            at = pl.multiple_of(i * chunk, 16)
            total = src[pl.ds(pl.multiple_of(base + me * size + at, 16), chunk), :].astype(F32)
            for d in range(1, n):
                total += landing[d - 1, pl.ds(at, chunk), :].astype(F32)
            dst[pl.ds(pl.multiple_of(dst_base + at, 16), chunk), :] = total.astype(BF)
            return 0

        if size == chunk:
            add(0, 0)
        else:
            lax.fori_loop(0, size // chunk, add, 0)

    def share(landing, me, n, peer):
        return [send(landing.at[me], landing.at[me], peer(d)) for d in far_first(n)]

    def summed_slots(landing, n):
        total = landing[0].astype(F32)
        for d in range(1, n):
            total += landing[d].astype(F32)
        return total

    def spread(ref, start, size, n, peer):
        return [
            send(rows(ref, start, size), rows(ref, start, size), peer(d)) for d in far_first(n)
        ]

    first_core = jnp.where(core == 0, 1.0, 0.0).astype(F32)

    def by_core(mine_if_first, mine_if_second):
        return first_core * mine_if_first + (1.0 - first_core) * mine_if_second

    for i in FIRST:
        fetch[i].wait()

    row_id = lax.broadcasted_iota(jnp.int32, (A, C), 0)
    alive = jnp.where(row_id < counts[0], 1.0, 0.0).astype(F32)
    masked32 = feat[...].astype(F32) * alive
    gm32 = cot[...].astype(F32) * alive
    masked, gm = masked32.astype(BF), gm32.astype(BF)
    for f in range(4):
        pick_t[:, f * 32 : (f + 1) * 32] = jnp.where(
            lax.broadcasted_iota(jnp.int32, (A, 32), 0) == ghost[f : f + 1, :], 1.0, 0.0
        )
    gout[...] = nn(pick_t[...].T.astype(BF), masked).astype(BF)
    x_out[...] = by_core(gm32, masked32).astype(BF)
    pos_out[...] = jnp.zeros_like(pos_out)
    pos_out[0:3, :] = pos[...]

    own_kind = by_core(masked32, gm32).astype(BF)
    kv[...] = jnp.zeros_like(kv)
    kv[0:3, :] = kvec[...] * (1.0 / (2.0 * math.pi))
    kv[3:4, :] = jnp.sqrt(kw[...] * factor_scale)

    def waves(turns, root):
        s, c = half_turns(turns - jnp.round(turns))
        s_root = s * root
        return (root - s * s_root).astype(BF), (c * s_root).astype(BF)

    def add_waves(first_row, place, start, stop):
        spots = [jnp.broadcast_to(place[a : a + 1, :], (A, A)).T for a in range(3)]
        spots = [jnp.concatenate([spot, spot], axis=1) for spot in spots]
        atoms = slice(first_row, first_row + A)

        def wave_block(block, _):
            at = pl.ds(pl.multiple_of(block * 256, 256), 256)
            turns = spots[0] * kv[0:1, at] + spots[1] * kv[1:2, at] + spots[2] * kv[2:3, at]
            cosine[atoms, at], sine[atoms, at] = waves(turns, kv[3:4, at])
            return 0

        lax.fori_loop(start // 256, stop // 256, wave_block, 0)

    add_waves(0, pos_out, 0, K)
    own_t = own_kind.astype(F32).T

    for i in LATER:
        fetch[i].wait()

    masked_t = masked32.T.astype(BF)

    src_t[...] = nn(masked, sw[...]).astype(BF).astype(F32).T
    ga_t[...] = nt(gm, mw[...]).astype(BF).astype(F32).T
    nbr_t[...] = nbr[...].astype(F32)
    s, c = half_turns(dist[...] * 0.1)
    gate_t[...] = jnp.where(nbr[...] < 2 * A, 0.5 * c * c, 0.0)
    tab_t[:, :A] = nn(masked, tw[...]).astype(BF).astype(F32).T.astype(BF)
    agg_t[...] = jnp.zeros_like(agg_t)
    gs_t[...] = jnp.zeros_like(gs_t)
    tsum[...] = jnp.zeros_like(tsum)
    epart[...] = jnp.zeros_like(epart)
    ew_t = ew[...].astype(F32).T.astype(BF)

    pl.semaphore_wait(barrier, len(greeted))
    atoms_in = [send(x_out, x_in, sibling), send(pos_out, pos_in, sibling)]
    ghosts_in = [
        send(gout.at[pl.ds(f * 32, 32)], gin.at[pl.ds(f * 32, 32)], faces[f]) for f in range(4)
    ]
    arrive(atoms_in)

    values_t = jnp.concatenate([own_t, x_in[...].astype(F32).T], axis=1).astype(BF)

    def sum_block(block, _):
        at = pl.ds(pl.multiple_of(block * 512, 512), 512)
        of_cos = nn(values_t, cosine[:, at]).astype(BF)
        of_sin = nn(values_t, sine[:, at]).astype(BF)
        sums[at, :C] = of_cos.T
        sums[at, C:] = of_sin.T
        return 0

    def add_sums(start, stop):
        add_waves(A, pos_in, start, stop)
        lax.fori_loop(start // 512, stop // 512, sum_block, 0)

    base_a, base_b, base_c = 0, ROWS[0], ROWS[0] + ROWS[1]
    a1, b1, c1 = ROWS[0] // nx, ROWS[1] // ny, ROWS[2] // nz
    a2, b2, c2 = a1 // ny, b1 // nx, c1 // nx
    add_sums(0, base_b)
    first_a = scatter(sums, base_a, la, x, nx, a1, x_peer)
    add_sums(base_b, base_c)
    first_b = scatter(sums, base_b, lb, y, ny, b1, y_peer)
    add_sums(base_c, K)
    first_c = scatter(sums, base_c, lc, z, nz, c1, z_peer)

    table_row = lax.broadcasted_iota(jnp.int32, (2 * A, A), 0).astype(F32).astype(BF)

    arrive(ghosts_in)
    ghosts = gin[...]
    tab_t[:, A:] = nn(ghosts, tw[...]).astype(BF).astype(F32).T.astype(BF)
    table_t = jnp.concatenate([masked_t, ghosts.astype(F32).T.astype(BF)], axis=1)

    def edge_step(step, _):
        slots = [(pl.ds(step * STEP + j, 1), slice(j * A, (j + 1) * A)) for j in range(STEP)]
        for row, at in slots:
            named = jnp.broadcast_to(nbr_t[row, :], (2 * A, A)).astype(BF)
            picks[:, at] = jnp.where(table_row == named, jnp.ones((), BF), jnp.zeros((), BF))
        summed = nn(tab_t[...], picks[...])
        for row, at in slots:
            v = summed[:, at] + src_t[...]
            g = 0.5 * jnp.tanh(0.5 * v) + 0.5
            hidden = v * g
            hiddens[:, at] = hidden.astype(BF)
            slopes[:, at] = g + hidden * (1.0 - g)
        mixed = nn(ew_t, hiddens[...])
        agg_sum = agg_t[...]
        for row, at in slots:
            v = mixed[:, at]
            g = 0.5 * jnp.tanh(0.5 * v) + 0.5
            message = v * g
            agg_sum += gate_t[row, :] * message
            inners[:, at] = (gate_t[row, :] * ga_t[...] * (g + message * (1.0 - g))).astype(BF)
        agg_t[...] = agg_sum
        outer = nn(ew[...], inners[...])
        gs_sum = gs_t[...]
        for row, at in slots:
            pair_grad = outer[:, at] * slopes[:, at]
            gs_sum += pair_grad
            pairs[:, at] = pair_grad.astype(BF)
        gs_t[...] = gs_sum
        epart[...] += nt(hiddens[...], inners[...])
        tsum[...] += nt(picks[...], pairs[...])
        return 0

    steps = NB // STEP
    lax.fori_loop(0, steps - 1, edge_step, 0)
    first_count = len(sent)
    arrive(first_a)
    collect(sums, base_a, la, x, nx, a1, ta)
    second_a = scatter(ta, 0, la2, y, ny, a2, y_peer)
    arrive(first_b)
    collect(sums, base_b, lb, y, ny, b1, tb)
    second_b = scatter(tb, 0, lb2, x, nx, b2, x_peer)
    arrive(first_c)
    collect(sums, base_c, lc, z, nz, c1, tc)
    second_c = scatter(tc, 0, lc2, x, nx, c2, x_peer)

    lax.fori_loop(steps - 1, steps, edge_step, 0)
    table_sum = tsum[...]
    aggregate_t = agg_t[...].astype(BF)
    grad_source = gs_t[...].T.astype(BF)
    g0[0:C, :] = nn(masked_t, grad_source).astype(BF)
    g0[C : 2 * C, :] = nn(table_t, table_sum.astype(BF)).astype(BF)
    g0[2 * C : 3 * C, :] = epart[...].astype(BF)
    g0[3 * C :, :] = nn(aggregate_t, gm).astype(BF)
    gx = 4 * C // (nx * nc)
    xc = x * nc + core
    g_x = [
        send(
            rows(g0, (ahead(x, d // nc, nx) * nc + ahead(core, d % nc, nc)) * gx, gx),
            rgx.at[d - 1],
            xc_peer(d),
        )
        for d in far_first(nx * nc)
    ]

    ggout[...] = table_sum[A:, :].astype(BF)
    ghosts_back = [
        send(ggout.at[pl.ds(f * 32, 32)], gret.at[pl.ds(f * 32, 32)], back[f]) for f in range(4)
    ]
    second_count = len(sent)
    ab2 = a2 + b2
    settle(first_count)
    arrive(second_b)
    collect(tb, 0, lb2, x, nx, b2, t2, a2)
    arrive(second_c)
    collect(tc, 0, lc2, x, nx, c2, t2, ab2)
    ly[pl.ds(y, 1)] = t2[ab2:, :][None]
    third_c = share(ly, y, ny, y_peer)
    arrive(second_a)
    collect(ta, 0, la2, y, ny, a2, t2, 0)
    lz[pl.ds(z, 1)] = t2[:ab2, :][None]
    third_ab = share(lz, z, nz, z_peer)

    arrive(g_x)
    collect(g0, 0, rgx, xc, nx * nc, gx, g1)
    rgy[pl.ds(y, 1)] = g1[...][None]
    g_y = share(rgy, y, ny, y_peer)

    arrive(ghosts_back)
    grad_target = (table_sum[:A, :] + nn(pick_t[...].astype(BF), gret[...])).astype(BF)
    short_grad = nt(grad_source, sw[...]) + nt(grad_target, tw[...])
    short_range = nn(agg_t[...].T.astype(BF), mw[...])

    fw_t = fw[...].astype(F32).T
    project = by_core(cw[...].astype(F32).T, fw_t).astype(BF)
    none = jnp.zeros((C, 64), BF)
    project = jnp.concatenate(
        [
            jnp.concatenate([project, none], axis=1),
            jnp.concatenate([none, project], axis=1),
        ],
        axis=0,
    )
    third_count = len(sent)
    settle(second_count)
    arrive(third_c)
    fin[ab2:, :] = summed_slots(ly, ny).astype(BF)
    arrive(third_ab)
    fin[:ab2, :] = summed_slots(lz, nz).astype(BF)
    w_out[...] = nn(fin[...], project).astype(BF)
    w_swap = [send(w_out, w_in, sibling)]
    place_a = pl.multiple_of(base_a + x * a1 + y * a2, 16)
    place_b = pl.multiple_of(base_b + y * b1 + x * b2, 16)
    place_c = pl.multiple_of(base_c + z * c1 + x * c2, 16)
    w_full[pl.ds(place_a, a2), :] = w_out[:a2, :]
    w_full[pl.ds(place_b, b2), :] = w_out[a2:ab2, :]
    w_full[pl.ds(place_c, c2), :] = w_out[ab2:, :]
    spread_a = spread(w_full, place_a, a2, ny, y_peer)
    spread_b = spread(w_full, place_b, b2, nx, x_peer)
    spread_c = spread(w_full, place_c, c2, nx, x_peer)

    arrive(w_swap)
    other_t = w_in[...].astype(F32).T
    in_ab = lax.broadcasted_iota(jnp.int32, other_t.shape, 1) < ab2

    def weight_part(left):
        quads = nn(left.astype(BF), fin[...])
        return (quads[:64, :C] + quads[64:, C:]).astype(BF)

    rhy[pl.ds(y, 1)] = weight_part(jnp.where(in_ab, other_t, 0.0))[None]
    rhz[pl.ds(z, 1)] = weight_part(jnp.where(in_ab, 0.0, other_t))[None]

    h_y = share(rhy, y, ny, y_peer)
    h_z = share(rhz, z, nz, z_peer)

    arrive(g_y)
    rgz[pl.ds(z, 1)] = summed_slots(rgy, ny).astype(BF)[None]
    g_z = share(rgz, z, nz, z_peer)

    settle(third_count)
    fourth_count = len(sent)
    arrive(spread_b)
    spread_b = spread(w_full, base_b + y * b1, b1, ny, y_peer)
    arrive(spread_c)
    spread_c = spread(w_full, base_c + z * c1, c1, nz, z_peer)
    arrive(spread_a)
    spread_a = spread(w_full, base_a + x * a1, a1, nx, x_peer)

    arrive(h_y)
    arrive(h_z)
    rhx[pl.ds(x, 1)] = (summed_slots(rhy, ny) + summed_slots(rhz, nz)).astype(BF)[None]
    h_x = share(rhx, x, nx, x_peer)

    arrive(g_z)
    g_mine = pl.multiple_of(xc * gx, 16)
    gfull[pl.ds(g_mine, gx), :] = summed_slots(rgz, nz).astype(BF)
    g_xs = spread(gfull, g_mine, gx, nx * nc, xc_peer)

    settle(fourth_count)

    def field_of(start, stop):
        at, weights = slice(start, stop), w_full[start:stop, :]
        return nn(cosine[:, at], weights), nn(sine[:, at], weights)

    arrive(spread_b)
    arrive(spread_c)
    of_cos, of_sin = field_of(base_b, K)
    arrive(spread_a)
    more_cos, more_sin = field_of(base_a, base_b)
    field = of_cos + more_cos + pltpu.roll(of_sin + more_sin, 64, 1)
    e_out[...] = field[A:, :].astype(BF)
    e_swap = [send(e_out, e_in, sibling)]
    field_here = field[:A, :]

    arrive(h_x)
    h2[...] = summed_slots(rhx, nx).astype(BF)
    h_swap = [send(h2, h_in, sibling)]

    arrive(e_swap)
    here = field_here.astype(BF).astype(F32)
    there = e_in[...].astype(F32)
    potential = by_core(here, there).astype(BF)[:, :64]
    grad_charge = by_core(there, here).astype(BF)[:, :64]
    out[0:A, :] = alive * (short_range + nn(potential, fw[...]))
    out[A : 2 * A, :] = alive * (short_grad + nn(grad_charge, cw[...]))

    arrive(h_swap)
    here, there = h2[...].astype(F32), h_in[...].astype(F32)
    out[6 * C : 6 * C + 64, :] = by_core(here, there) * grad_scale
    out[6 * C + 64 : 7 * C, :] = by_core(there, here) * grad_scale

    arrive(g_xs)
    out[2 * C : 6 * C, :] = gfull[...].astype(F32) * grad_scale

    settle(len(sent))


def place(
    rows, o_layer, o_feat, o_sg, o_tg, o_eg, o_mg, o_cg, o_fg, layer, feat, sem
):
    layer[...] = rows[0:A, :].astype(BF)
    feat[...] = rows[A : 2 * A, :].astype(BF)
    moves = [(layer, o_layer), (feat, o_feat)]
    moves += [
        (rows.at[pl.ds((i + 2) * C, C)], out) for i, out in enumerate((o_sg, o_tg, o_eg, o_mg))
    ]
    moves += [(rows.at[pl.ds(6 * C, 64)], o_cg), (rows.at[pl.ds(6 * C + 64, 64)], o_fg)]
    copies = [pltpu.make_async_copy(a, b, sem.at[i]) for i, (a, b) in enumerate(moves)]
    for copy in copies:
        copy.start()
    for copy in copies:
        copy.wait()


def local(
    features, positions, neighbours, distances, ghost_rows, atom_counts, wavevectors,
    wave_weights, source_weight, target_weight, edge_weight, mix_weight, charge_weight,
    field_weight, cotangent,
):
    geo = GEOMETRY
    nx, ny, nc, nz = geo["x"], geo["y"], geo["core"], geo["z_lo"] * geo["z_hi"]
    total_atoms = A * lax.axis_size("dx") * lax.axis_size("dy")
    factor_scale = 4.0 / math.sqrt(total_atoms * K)
    grad_scale = 1.0 / math.sqrt(total_atoms)
    a1, b1, c1 = ROWS[0] // nx, ROWS[1] // ny, ROWS[2] // nz
    a2, b2, c2 = a1 // ny, b1 // nx, c1 // nx
    last = a2 + b2 + c2
    gx = 4 * C // (nx * nc)

    def bf(*shape):
        return pltpu.VMEM(shape, BF)

    def f32(*shape):
        return pltpu.VMEM(shape, F32)

    scratch = [
        bf(A, C), bf(A, C), f32(8, A), f32(8, A), f32(8, K), bf(K, 2 * C),
        bf(nx - 1, a1, 2 * C), bf(a1, 2 * C),
        bf(ny - 1, b1, 2 * C), bf(b1, 2 * C),
        bf(nz - 1, c1, 2 * C), bf(c1, 2 * C),
        bf(ny - 1, a2, 2 * C), bf(nx - 1, b2, 2 * C), bf(nx - 1, c2, 2 * C),
        bf(last, 2 * C), bf(nz, a2 + b2, 2 * C), bf(ny, c2, 2 * C), bf(last, 2 * C),
        bf(last, C), bf(last, C), bf(K, C), bf(2 * A, K), bf(2 * A, K), bf(A, C), bf(A, C),
        bf(A, C), bf(A, C), bf(A, C), bf(A, C),
        bf(4 * C, C), bf(nx * nc - 1, gx, C), bf(gx, C), bf(ny, gx, C), bf(nz, gx, C),
        bf(4 * C, C),
        bf(ny, 64, C), bf(nz, 64, C), bf(nx, 64, C), bf(64, C), bf(64, C),
        bf(2 * A, STEP * A), bf(C, STEP * A), f32(C, STEP * A),
        bf(C, STEP * A), bf(C, STEP * A),
        f32(NB, A), f32(NB, A), f32(C, A), f32(C, A), bf(C, 2 * A), f32(A, A),
        f32(C, A), f32(C, A), f32(2 * A, C), f32(C, C),
        pltpu.SemaphoreType.DMA((COPIES,)),
        pltpu.SemaphoreType.DMA((COPIES,)),
    ]
    vmem = pl.BlockSpec(memory_space=pltpu.VMEM)
    anywhere = pl.BlockSpec(memory_space=pl.ANY)
    operands = (
        features, positions, neighbours.T, distances.T, ghost_rows, atom_counts, wavevectors,
        wave_weights.reshape(1, K), source_weight, target_weight, edge_weight, mix_weight,
        charge_weight.T, field_weight, cotangent,
    )
    n_in = len(operands)
    held = [
        pltpu.SMEM(a.shape, a.dtype) if a.ndim == 1 else pltpu.VMEM(a.shape, a.dtype)
        for a in operands
    ]

    def kernel(*refs):
        left = refs[n_in + 1 :]
        body(factor_scale, grad_scale, refs[:n_in], refs[n_in], left[:n_in], *left[n_in:])

    rows = pl.pallas_call(
        kernel,
        out_shape=jax.ShapeDtypeStruct((7 * C, C), F32),
        in_specs=[anywhere] * n_in,
        out_specs=vmem,
        scratch_shapes=held + [pltpu.SemaphoreType.DMA((n_in,))] + scratch,
        compiler_params=pltpu.CompilerParams(
            collective_id=0, has_side_effects=True, vmem_limit_bytes=60 * 1024 * 1024
        ),
        name="ewald_layer",
    )(*operands)
    outs = pl.pallas_call(
        place,
        out_shape=[jax.ShapeDtypeStruct((A, C), BF)] * 2
        + [jax.ShapeDtypeStruct((C, C), F32)] * 4
        + [jax.ShapeDtypeStruct((64, C), F32)] * 2,
        in_specs=[vmem],
        out_specs=[anywhere] * 8,
        scratch_shapes=[bf(A, C), bf(A, C), pltpu.SemaphoreType.DMA((8,))],
        name="place_outputs",
    )(rows)
    return (*outs[:6], outs[6].T, outs[7])


def solution(mesh):
    atoms = P(("dx", "dy"), None)
    in_specs = (
        atoms, P(None, ("dx", "dy")), atoms, atoms, P(None, ("dx", "dy")), P(("dx", "dy")),
        P(), P(), P(), P(), P(), P(), P(), P(), atoms,
    )
    out_specs = (atoms, atoms, P(), P(), P(), P(), P(), P())
    return jax.shard_map(
        local, mesh=mesh, in_specs=in_specs, out_specs=out_specs, check_vma=False
    )
```
